256 devices in a mesh: space: 32 (over y, x, core), dp: 8 (over z).
Axes of the slice: x: 4, y: 4, z: 8, core: 2. Of those that a mesh axis runs over, the one named last changes fastest.
Arguments:
- features: bfloat16 [8, 32, 512, 256], P('dp', 'space'), may hold values from -6 to 6
- grad_out: bfloat16 [8, 32, 512, 256], P('dp', 'space'), may hold values from -6 to 6
- weight: bfloat16 [27, 256, 256], replicated, may hold values from -0.078125 to 0.078125
- neighbours: int32 [8, 32, 27], P('dp', 'space'), may hold values from -1 to 31, as said below
Outputs:
- conv_out: bfloat16 [8, 32, 512, 256], P('dp', 'space')
- grad_in: bfloat16 [8, 32, 512, 256], P('dp', 'space')
- grad_weight: float32 [6912, 256], P('dp')
The draws below stay inside these ranges and needn't reach their ends.
Inputs may be any that keep to these rules, and one draw needn't show every extreme that they name: Each scene's occupied bricks lie in a corridor two bricks wide in x and y, taken in the order z * 4 + y * 2 + x and given in that order to the slots, device by device along space; every device holds exactly one brick slot, and it is occupied. An entry names a slot of the same scene; neighbours are symmetric (slot m at offset k of slot n means slot n at offset 26 - k of slot m), offset 13 of an occupied slot is the slot itself, and a neighbour's device differs from the slot's device by at most 7 along space.
All inputs are finite; a program needn't handle non-finite values.
Results may differ from the reference program's by a relative error of at most 0.001.
Values may be sent and summed in bfloat16 or wider, within the bound.
No kernel may reach another device: no remote copies, remote signals or barrier semaphores. Data moves between devices by JAX's collectives and lax.ppermute only.
A program may use at most 128 MiB of HBM per device.

```python
import math
import jax
import jax.numpy as jnp
from jax import lax

C = 256
BD = 1
VOX = 512
TAPS = 27
NB = 32
SCENES = 8
N_SPACE = 32
N_DP = 8


def draw_scene(key):
    key_count, key_gap = jax.random.split(key)
    live_count = jax.random.randint(key_count, (N_SPACE,), 1, BD + 1).astype(jnp.int32)
    live_count = live_count.at[0].set(BD)
    live_count = live_count.at[N_SPACE - 1].set(BD)
    first_rank = jnp.cumsum(live_count) - live_count
    cell_gaps = jax.random.randint(key_gap, (NB,), 1, 3).astype(jnp.int32)
    cell_of_rank = jnp.cumsum(cell_gaps) - 1
    slot_ids = jnp.arange(NB, dtype=jnp.int32)
    owner_dev = slot_ids // BD
    within = slot_ids % BD
    is_live = within < live_count[owner_dev]
    rank_now = jnp.minimum(first_rank[owner_dev] + within, NB - 1)
    cell_now = cell_of_rank[rank_now]
    cell_limit = 2 * NB + 8
    lookup = jnp.full((cell_limit,), -1, jnp.int32)
    lookup = lookup.at[jnp.where(is_live, cell_now, cell_limit)].set(slot_ids, mode='drop')
    along_x = cell_now % 2
    along_y = cell_now // 2 % 2
    along_z = cell_now // 4
    shifts = jnp.arange(3, dtype=jnp.int32) - 1
    off_x = jnp.repeat(shifts, 9)
    off_y = jnp.tile(jnp.repeat(shifts, 3), 3)
    off_z = jnp.tile(shifts, 9)
    target_x = along_x[:, None] + off_x[None]
    target_y = along_y[:, None] + off_y[None]
    target_z = along_z[:, None] + off_z[None]
    inside = (target_x >= 0) & (target_x < 2) & (target_y >= 0) & (target_y < 2) & (target_z >= 0)
    target = jnp.clip(target_z * 4 + target_y * 2 + target_x, 0, cell_limit - 1)
    found = lookup[target]
    return jnp.where(inside & is_live[:, None], found, -1).astype(jnp.int32)


def draw_neighbours(key, part):
    key = jax.random.fold_in(key, 5)
    return jax.vmap(draw_scene)(jax.random.split(key, N_DP))


def block_scale(own_key, shape, cuts, low, largest):
    def one(dim, parts):
        heights = jax.random.uniform(jax.random.fold_in(jax.random.fold_in(own_key, 6), dim), (parts,), jnp.float32, low / len(cuts), largest / len(cuts))
        return jnp.repeat(jnp.exp(heights), shape[dim] // parts).reshape((-1,) + (1,) * (len(shape) - dim - 1))

    gain = one(*cuts[0])
    for cut in cuts[1:]:
        gain = gain * one(*cut)
    return gain


def centred(stream_key, extent, deviation, limit, cuts=(), kind=jnp.bfloat16):
    values = deviation * jax.random.normal(stream_key, extent, jnp.float32)
    if cuts:
        values = values * block_scale(stream_key, extent, cuts, -0.22, 0.18)
    return jnp.clip(values, -limit, limit).astype(kind)


def setup_inputs(seed: int = 0) -> dict:
    keys = jax.random.split(jax.random.key(seed), 5)
    return {
        "features": centred(keys[0], (SCENES, NB, VOX, C), 1.0, 6.0, ((0, 8), (1, 32))),
        "grad_out": centred(keys[1], (SCENES, NB, VOX, C), 1.0, 6.0, ((0, 8), (1, 32))),
        "weight": centred(keys[2], (TAPS, C, C), (TAPS * C) ** -0.5, 0.078125),
        "neighbours": draw_neighbours(jax.random.fold_in(keys[4], 71), 0),
    }


def assemble(tile_set):
    brick_count = tile_set.shape[0]
    channels = tile_set.shape[-1]
    tile_set = tile_set.reshape(brick_count, 3, 3, 3, 8, 8, 8, channels)
    for axis_step in range(3):
        tile_set = jnp.concatenate([tile_set[:, 0, :, :, 7:8], tile_set[:, 1], tile_set[:, 2, :, :, 0:1]], axis=3)
    return tile_set

def windows(padded, flipped):
    channels = padded.shape[-1]
    columns = []
    for i in range(3):
        for j in range(3):
            for l in range(3):
                start_x, start_y, start_z = (2 - i, 2 - j, 2 - l) if flipped else (i, j, l)
                piece = padded[:, start_x:start_x + 8, start_y:start_y + 8, start_z:start_z + 8, :]
                columns.append(piece.reshape(-1, channels))
    return jnp.concatenate(columns, axis=1)

def reference(features, grad_out, weight, neighbours):
    channels = features.shape[-1]
    flat_x = features.reshape(N_DP * NB, VOX, channels)
    flat_y = grad_out.reshape(N_DP * NB, VOX, channels)
    offsets = (jnp.arange(N_DP, dtype=jnp.int32) * NB)[:, None, None]
    link_table = jnp.where(neighbours >= 0, neighbours + offsets, -1).astype(jnp.int32).reshape(N_DP * NB, TAPS)
    stacked_w = weight.reshape(TAPS * channels, channels)
    flipped_w = jnp.transpose(weight, (0, 2, 1)).reshape(TAPS * channels, channels)
    grad_scale = 1.0 / math.sqrt(N_DP * NB * VOX)

    def fetch_tiles(table, link_row):
        is_live = link_row >= 0
        tile_set = table[jnp.where(is_live, link_row, 0)]
        return jnp.where(is_live[:, None, None], tile_set, jnp.zeros_like(tile_set))

    def per_brick(accum_w, scan_item):
        brick_index, link_row = scan_item
        padded_in = assemble(fetch_tiles(flat_x, link_row)[None])
        padded_cot = assemble(fetch_tiles(flat_y, link_row)[None])
        stack_x = windows(padded_in, False)
        conv_out = jnp.dot(stack_x, stacked_w, preferred_element_type=jnp.float32).astype(jnp.bfloat16)
        grad_in = jnp.dot(windows(padded_cot, True), flipped_w, preferred_element_type=jnp.float32).astype(jnp.bfloat16)
        own_cot = flat_y[brick_index]
        accum_w = accum_w + jnp.dot(stack_x.T, own_cot, preferred_element_type=jnp.float32)
        return (accum_w, (conv_out, grad_in))
    start_w = jnp.zeros((TAPS * channels, channels), jnp.float32)
    brick_ids = jnp.arange(N_DP * NB, dtype=jnp.int32)
    accum_w, (outs, grads) = lax.scan(per_brick, start_w, (brick_ids, link_table))
    return (outs.reshape(features.shape), grads.reshape(features.shape), accum_w * grad_scale)
```

```python
import functools
import math

import jax
import jax.numpy as jnp
from jax import lax
from jax.experimental import pallas as pl
from jax.experimental.pallas import tpu as pltpu
from jax.sharding import PartitionSpec as P

f32 = jnp.float32
bf16 = jnp.bfloat16
i16 = jnp.int16
i32 = jnp.int32

SPACE = 32
SCENES = 8
CHIPS = 16
HALF = 128
LEVELS = 32766.0
VMEM_LIMIT = 56 * 1024 * 1024

OFFSETS = [(k, k // 9 - 1, k // 3 % 3 - 1, k % 3 - 1) for k in range(27) if k != 13]


def vmem():
    return pl.BlockSpec(memory_space=pltpu.VMEM)


def smem():
    return pl.BlockSpec(memory_space=pltpu.SMEM)


def hbm():
    return pl.BlockSpec(memory_space=pl.ANY)


def side(shift):
    return 7 if shift > 0 else 0


def region(ref, shifts):
    dx, dy, dz = shifts
    kinds = (dx != 0, dy != 0, dz != 0)
    if kinds == (True, False, False):
        return ref[pl.ds(side(dx) * 64, 64), :]
    if kinds == (False, True, False):
        return jnp.concatenate([ref[pl.ds(x * 64 + side(dy) * 8, 8), :] for x in range(8)], axis=0)
    if kinds == (False, False, True):
        return ref[pl.ds(side(dz), 64, stride=8), :]
    if kinds == (True, True, False):
        rows = ref[pl.ds(side(dx) * 64 + side(dy) * 8, 8), :]
    elif kinds == (True, False, True):
        rows = ref[pl.ds(side(dx) * 64 + side(dz), 8, stride=8), :]
    elif kinds == (False, True, True):
        rows = ref[pl.ds(side(dy) * 8 + side(dz), 8, stride=64), :]
    else:
        row = ref[pl.ds(side(dx) * 64 + side(dy) * 8 + side(dz), 1), :]
        rows = jnp.broadcast_to(row, (8, HALF))
    return jnp.concatenate([rows, rows], axis=0)


def pack_kernel(own_ref, links_ref, x_ref, c_ref, out_ref, pair_ref, parts):
    core = lax.rem(own_ref[0], 2)
    for half in range(2):
        lanes = pl.ds(half * HALF, HALF)
        parts[2 * half] = x_ref[:, lanes].astype(f32)
        parts[2 * half + 1] = c_ref[:, lanes].astype(f32)
    pair_ref[:, 0:256] = x_ref[...]

    @pl.when(core == 0)
    def _():
        pair_ref[:, 256:384] = c_ref[:, 128:256]

    @pl.when(core == 1)
    def _():
        pair_ref[:, 256:384] = c_ref[:, 0:128]

    for k, *shifts in OFFSETS:
        target = links_ref[k]

        @pl.when(target >= 0)
        def _(target=target, shifts=tuple(shifts)):
            chip = target // 2
            brick = lax.rem(target, 2)
            for half in range(2):
                for tensor in range(2):
                    rows = region(parts.at[2 * half + tensor], shifts)
                    count = rows.shape[0]
                    out_ref[2 * chip + half, brick, 0:count, tensor * HALF : (tensor + 1) * HALF] = rows.astype(bf16)


def pack(own, links, x, c):
    return pl.pallas_call(
        pack_kernel,
        out_shape=(
            jax.ShapeDtypeStruct((SPACE, 2, 64, 256), bf16),
            jax.ShapeDtypeStruct((512, 384), bf16),
        ),
        in_specs=[smem(), smem(), vmem(), vmem()],
        out_specs=(vmem(), vmem()),
        scratch_shapes=[pltpu.VMEM((4, 512, HALF), f32)],
        compiler_params=pltpu.CompilerParams(vmem_limit_bytes=VMEM_LIMIT),
    )(own, links, x, c)


def target_plane(shift):
    return 9 if shift > 0 else 0


def quantise(values, peak):
    code = jnp.ceil(jnp.log2(jnp.maximum(peak, 2.0**-110)) * 256.0) + 1.0
    factor = LEVELS * jnp.exp2(code * (-1.0 / 256.0))
    return jnp.round(values * factor).astype(i32).astype(i16), code


def code_rows(code):
    return jnp.broadcast_to(code, (16, HALF)).astype(i32).astype(i16)


def step_of(code_row):
    return jnp.exp2(code_row * (1.0 / 256.0)) * (1.0 / LEVELS)


def fill(brick, links_ref, halo_ref, tensor, own_rows, plane, low, high, shifted_low, shifted_high, padded):
    lanes = slice(tensor * HALF, (tensor + 1) * HALF)
    plane[...] = jnp.zeros_like(plane)
    low[...] = jnp.zeros_like(low)
    high[...] = jnp.zeros_like(high)
    for x in range(8):
        plane[pl.ds((x + 1) * 80 + 8, 64), :] = own_rows(x * 64)
    for k, dx, dy, dz in OFFSETS:
        source = links_ref[k]

        @pl.when(source >= 0)
        def _(source=source, dx=dx, dy=dy, dz=dz):
            at_x, at_y = target_plane(dx), target_plane(dy)
            face = (dx != 0) + (dy != 0) + (dz != 0) == 1
            got = halo_ref[source, brick, 0 : 64 if face else 16, lanes].astype(f32)
            if dz == 0:
                if dy == 0:
                    plane[pl.ds(at_x * 80 + 8, 64), :] = got
                elif dx == 0:
                    for x in range(8):
                        plane[pl.ds((x + 1) * 80 + at_y * 8, 8), :] = got[x * 8 : x * 8 + 8]
                else:
                    plane[pl.ds(at_x * 80 + at_y * 8, 8), :] = got[0:8]
            else:
                rim = low if dz < 0 else high
                if dx == 0 and dy == 0:
                    for x in range(8):
                        rim[pl.ds((x + 1) * 10 + 1, 8), :] = got[x * 8 : x * 8 + 8]
                elif dy == 0:
                    rim[pl.ds(at_x * 10 + 1, 8), :] = got[0:8]
                elif dx == 0:
                    rim[pl.ds(10 + at_y, 8, stride=10), :] = got[0:8]
                else:
                    rim[pl.ds(at_x * 10 + at_y, 1), :] = got[0:1]

    shifted_low[pl.ds(1, 800), :] = plane[pl.ds(0, 800), :]
    shifted_low[pl.ds(0, 104, stride=8), :] = low[...]
    shifted_high[pl.ds(0, 800), :] = plane[pl.ds(1, 800), :]
    shifted_high[pl.ds(7, 104, stride=8), :] = high[...]
    for j in range(3):
        for l, source in enumerate((shifted_low, plane, shifted_high)):
            at = (3 * j + l) * HALF
            for x in range(10):
                padded[tensor, brick, x * 64 : x * 64 + 64, at : at + HALF] = source[
                    pl.ds(x * 80 + j * 8, 64), :
                ].astype(bf16)


def main_kernel(
    own_ref, links_ref, mate_links_ref, x_ref, c_ref, pair_ref, halo_ref, weight_ref,
    sums_ref, terms_ref,
    plane, low, high, shifted_low, shifted_high, padded, x_turned, grads, w_in, w_out, sems,
):
    core = lax.rem(own_ref[0], 2)
    start = pl.multiple_of(core * HALF, HALF)
    copies = [
        pltpu.make_async_copy(weight_ref.at[:, pl.ds(start, HALF), :], w_in, sems.at[0])
    ]
    for kk in range(27):
        copies.append(
            pltpu.make_async_copy(
                weight_ref.at[26 - kk, :, pl.ds(start, HALF)],
                w_out.at[:, pl.ds(kk * HALF, HALF)],
                sems.at[1 + kk],
            )
        )
    for copy in copies:
        copy.start()

    def assemble(brick, links, rows_of):
        for tensor in range(2):
            fill(brick, links, halo_ref, tensor, rows_of[tensor], plane, low, high, shifted_low, shifted_high, padded)

    def own_rows(ref, at):
        def rows(first):
            return ref[pl.ds(first, 64), at : at + HALF].astype(f32)

        return rows

    for here in range(2):

        @pl.when(core == here)
        def _(here=here):
            at = here * HALF
            assemble(here, links_ref, (own_rows(x_ref, at), own_rows(c_ref, at)))
            assemble(1 - here, mate_links_ref, (own_rows(pair_ref, at), own_rows(pair_ref, 256)))
            x_turned[here] = x_ref[...].T
            x_turned[1 - here] = pair_ref[:, 0:256].T

    for i in range(3):
        window = slice(i * 64, i * 64 + 512)
        term = jnp.dot(x_turned[0], padded[1, 0, window, :], preferred_element_type=f32)
        term += jnp.dot(x_turned[1], padded[1, 1, window, :], preferred_element_type=f32)
        for jl in range(9):
            grads[26 - (9 * i + jl)] = term[:, jl * HALF : (jl + 1) * HALF]
    for q in range(CHIPS):
        rows = slice(q * 16, q * 16 + 16)
        peak = jnp.abs(grads[0, rows, :])
        for k in range(1, 27):
            peak = jnp.maximum(peak, jnp.abs(grads[k, rows, :]))
        peak = jnp.max(peak, axis=0, keepdims=True)
        coded, code = quantise(grads[:, rows, :].reshape(432, HALF), peak)
        terms_ref[q, 0:432, :] = coded
        terms_ref[q, 432:448, :] = code_rows(code)

    for copy in copies:
        copy.wait()
    for brick in range(2):
        for part in range(2):
            total = jnp.zeros((512, 256), f32)
            for i in range(3):
                block = padded[part, brick, i * 64 : i * 64 + 512, :]
                if part == 0:
                    taps = w_in[9 * i : 9 * i + 9].reshape(9 * HALF, 256)
                    total += jnp.dot(block, taps, preferred_element_type=f32)
                else:
                    taps = w_out[:, i * 9 * HALF : (i + 1) * 9 * HALF]
                    total += lax.dot_general(block, taps, (((1,), (1,)), ((), ())), preferred_element_type=f32)
            sums_ref[lax.rem(core + brick, 2), part] = total


def main(own, links, mate_links, x, c, pair, halo, weight):
    return pl.pallas_call(
        main_kernel,
        out_shape=(
            jax.ShapeDtypeStruct((2, 2, 512, 256), f32),
            jax.ShapeDtypeStruct((CHIPS, 448, HALF), i16),
        ),
        in_specs=[smem(), smem(), smem(), vmem(), vmem(), vmem(), vmem(), hbm()],
        out_specs=(vmem(), vmem()),
        scratch_shapes=[
            pltpu.VMEM((832, HALF), f32),
            pltpu.VMEM((104, HALF), f32),
            pltpu.VMEM((104, HALF), f32),
            pltpu.VMEM((832, HALF), f32),
            pltpu.VMEM((832, HALF), f32),
            pltpu.VMEM((2, 2, 640, 9 * HALF), bf16),
            pltpu.VMEM((2, 256, 512), bf16),
            pltpu.VMEM((27, 256, HALF), f32),
            pltpu.VMEM((27, HALF, 256), bf16),
            pltpu.VMEM((256, 27 * HALF), bf16),
            pltpu.SemaphoreType.DMA((28,)),
        ],
        compiler_params=pltpu.CompilerParams(vmem_limit_bytes=VMEM_LIMIT),
    )(own, links, mate_links, x, c, pair, halo, weight)


def scene_kernel(own_ref, got_ref, out_ref, total):
    chip = own_ref[0] // 2
    steps = [step_of(got_ref[source, 432:448, :].astype(i32).astype(f32)) for source in range(CHIPS)]
    for k in range(27):
        unit = jnp.zeros((16, HALF), f32)
        for source in range(CHIPS):
            unit += got_ref[source, k * 16 : k * 16 + 16, :].astype(i32).astype(f32) * steps[source]
        total[k] = unit
    total[27] = jnp.zeros((16, HALF), f32)
    for scene in range(SCENES):
        rest = lax.rem(chip - 6 * scene + 96, 16)
        first = (54 * scene + rest - chip) // 16
        units = [total[jnp.minimum(first + t, 27)] for t in range(4)]
        peak = jnp.abs(units[0])
        for unit in units[1:]:
            peak = jnp.maximum(peak, jnp.abs(unit))
        peak = jnp.max(peak, axis=0, keepdims=True)
        for t in range(4):
            coded, code = quantise(units[t], peak)
            out_ref[scene, t * 16 : t * 16 + 16, :] = coded
        out_ref[scene, 64:80, :] = code_rows(code)


def scene_sum(own, got):
    return pl.pallas_call(
        scene_kernel,
        out_shape=jax.ShapeDtypeStruct((SCENES, 80, HALF), i16),
        in_specs=[smem(), vmem()],
        out_specs=vmem(),
        scratch_shapes=[pltpu.VMEM((28, 16, HALF), f32)],
        compiler_params=pltpu.CompilerParams(vmem_limit_bytes=VMEM_LIMIT),
    )(own, got)


def whole_kernel(scale, got_ref, out_ref):
    total = jnp.zeros((64, HALF), f32)
    for scene in range(SCENES):
        step = step_of(got_ref[scene, 64:80, :].astype(i32).astype(f32))
        total += got_ref[scene, 0:64, :].astype(i32).astype(f32) * step[0:1]
    total *= scale
    peak = jnp.max(jnp.abs(total), axis=0, keepdims=True)
    coded, code = quantise(total, peak)
    codes = code_rows(code)
    for target in range(SPACE):
        out_ref[target, 0:64, :] = coded
        out_ref[target, 64:80, :] = codes


def whole_sum(scale, got):
    return pl.pallas_call(
        functools.partial(whole_kernel, scale),
        out_shape=jax.ShapeDtypeStruct((SPACE, 80, HALF), i16),
        in_specs=[vmem()],
        out_specs=vmem(),
        compiler_params=pltpu.CompilerParams(vmem_limit_bytes=VMEM_LIMIT),
    )(got)


def place_kernel(own_ref, got_ref, out_ref):
    scene = own_ref[1]
    for chip in range(CHIPS):
        rest = lax.rem(chip - 6 * scene + 96, 16)
        for half in range(2):
            lanes = slice(half * HALF, (half + 1) * HALF)
            source = 2 * chip + half
            step = step_of(got_ref[source, 64:80, :].astype(i32).astype(f32))
            for t in range(4):
                values = got_ref[source, t * 16 : t * 16 + 16, :].astype(i32).astype(f32) * step
                if t < 3:
                    out_ref[pl.ds(pl.multiple_of((16 * t + rest) * 16, 16), 16), lanes] = values
                else:

                    @pl.when(rest < 6)
                    def _(values=values, t=t, rest=rest, lanes=lanes):
                        out_ref[pl.ds(pl.multiple_of((16 * t + rest) * 16, 16), 16), lanes] = values


def place(own, got):
    return pl.pallas_call(
        place_kernel,
        out_shape=jax.ShapeDtypeStruct((864, 256), f32),
        in_specs=[smem(), vmem()],
        out_specs=vmem(),
        compiler_params=pltpu.CompilerParams(vmem_limit_bytes=VMEM_LIMIT),
    )(own, got)


def body(features, grad_out, weight, neighbours):
    x = features[0, 0]
    c = grad_out[0, 0]
    links = neighbours[0, 0]
    own = jnp.stack([lax.axis_index("space"), lax.axis_index("dp")]).astype(i32)
    mates = [(i, i ^ 1) for i in range(SPACE)]
    same_core = [[2 * q + core for q in range(CHIPS)] for core in range(2)]
    grad_scale = 1.0 / math.sqrt(SCENES * SPACE * 512)

    mate_links = lax.ppermute(links, "space", mates)
    outgoing, pair = pack(own, links, x, c)
    pair = lax.ppermute(pair, "space", mates)
    halo = lax.all_to_all(outgoing, "space", 0, 0, tiled=True)
    sums, terms = main(own, links, mate_links, x, c, pair, halo, weight)
    mate_sums = lax.ppermute(sums[1], "space", mates)
    terms = lax.all_to_all(terms, "space", 0, 0, tiled=True, axis_index_groups=same_core)
    scene_terms = lax.all_to_all(scene_sum(own, terms), "dp", 0, 0, tiled=True)
    whole = lax.all_to_all(whole_sum(grad_scale, scene_terms), "space", 0, 0, tiled=True)
    grad_weight = place(own, whole)
    both = (sums[0] + mate_sums).astype(bf16)
    return both[0][None, None], both[1][None, None], grad_weight


def solution(mesh):
    placed = (
        P("dp", "space", None, None),
        P("dp", "space", None, None),
        P(),
        P("dp", "space", None),
    )
    return jax.shard_map(
        body,
        mesh=mesh,
        in_specs=placed,
        out_specs=(P("dp", "space", None, None), P("dp", "space", None, None), P("dp", None)),
        check_vma=False,
    )
```

```python
import functools
import math

import jax
import jax.numpy as jnp
from jax import lax
from jax.experimental import pallas as pl
from jax.experimental.pallas import tpu as pltpu
from jax.sharding import PartitionSpec as P

f32 = jnp.float32
bf16 = jnp.bfloat16
i16 = jnp.int16
i32 = jnp.int32

SPACE = 32
LG, LS, LW, LP = 51, 50, 50, 51

SCENES = 8
CHIPS = 16
HALF = 128
LEVELS = 32766.0

FAR = 3
HOPS = (-2, -1, 1, 2)

OFFSETS = [(k, k // 9 - 1, k // 3 % 3 - 1, k % 3 - 1) for k in range(27) if k != 13]


def position():
    return lax.axis_index("space"), lax.axis_index("dp")


def params(mib):
    return pltpu.CompilerParams(vmem_limit_bytes=mib << 20)


def cost(us):
    return pl.CostEstimate(flops=int(us * 1e9), bytes_accessed=1 << 20, transcendentals=0)


def vmem():
    return pl.BlockSpec(memory_space=pltpu.VMEM)


def smem():
    return pl.BlockSpec(memory_space=pltpu.SMEM)


def hbm():
    return pl.BlockSpec(memory_space=pltpu.HBM)


def anywhere():
    return pl.BlockSpec(memory_space=pl.ANY)


def side(shift):
    return 7 if shift > 0 else 0


def region(ref, shifts):
    dx, dy, dz = shifts
    kinds = (dx != 0, dy != 0, dz != 0)
    if kinds == (True, False, False):
        return ref[pl.ds(side(dx) * 64, 64), :]
    if kinds == (False, True, False):
        return jnp.concatenate([ref[pl.ds(x * 64 + side(dy) * 8, 8), :] for x in range(8)], axis=0)
    if kinds == (False, False, True):
        return ref[pl.ds(side(dz), 64, stride=8), :]
    if kinds == (True, True, False):
        rows = ref[pl.ds(side(dx) * 64 + side(dy) * 8, 8), :]
    elif kinds == (True, False, True):
        rows = ref[pl.ds(side(dx) * 64 + side(dz), 8, stride=8), :]
    elif kinds == (False, True, True):
        rows = ref[pl.ds(side(dy) * 8 + side(dz), 8, stride=64), :]
    else:
        row = ref[pl.ds(side(dx) * 64 + side(dy) * 8 + side(dz), 1), :]
        rows = jnp.broadcast_to(row, (8, HALF))
    return jnp.concatenate([rows, rows], axis=0)


def pack_kernel(links_ref, x_ref, c_ref, out_ref, parts):
    chip = position()[0] // 2
    for half in range(2):
        lanes = slice(half * HALF, (half + 1) * HALF)
        parts[half] = c_ref[:, lanes].astype(f32)
        parts[2 + half] = x_ref[:, lanes].astype(f32)
    for k, *shifts in OFFSETS:
        target = links_ref[k]

        @pl.when(target >= 0)
        def _(target=target, shifts=tuple(shifts)):
            to = target // 2
            brick = lax.rem(target, 2)
            for half in range(2):
                rows = region(parts.at[half], shifts)
                out_ref[2 * to + half, brick, 0 : rows.shape[0], :] = rows.astype(bf16)
            if sum(map(abs, shifts)) > 1:

                @pl.when(jnp.abs(to - chip) >= FAR)
                def _():
                    for half in range(2):
                        out_ref[2 * to + half, brick, 16:32, :] = region(parts.at[2 + half], shifts).astype(bf16)


def pack(links, x, c):
    return pl.pallas_call(
        pack_kernel,
        out_shape=jax.ShapeDtypeStruct((SPACE, 2, 64, HALF), bf16),
        in_specs=[smem(), vmem(), vmem()],
        out_specs=vmem(),
        scratch_shapes=[pltpu.VMEM((4, 512, HALF), f32)],
        compiler_params=params(56),
    )(links, x, c)


def pair_kernel(x_ref, c_ref, _, out_ref):
    core = lax.rem(position()[0], 2)
    out_ref[:, 0:256] = x_ref[...]
    for here in range(2):

        @pl.when(core == here)
        def _(here=here):
            out_ref[:, 256:384] = c_ref[:, (1 - here) * HALF : (2 - here) * HALF]


def pair_rows(x, c, after):
    return pl.pallas_call(
        pair_kernel,
        out_shape=jax.ShapeDtypeStruct((512, 384), bf16),
        in_specs=[vmem(), vmem(), anywhere()],
        out_specs=vmem(),
        compiler_params=params(56),
        cost_estimate=cost(1.0),
    )(x, c, after)


def prepare_kernel(links_ref, mate_links_ref, x_ref, c_ref, pair_ref, *rest):
    outs, turned_ref, x_half_ref, c_half_ref, parts, slots, sems = rest[:5], *rest[5:]
    own = position()[0]
    core = lax.rem(own, 2)
    chip = own // 2
    mate = 1 - core
    for here in range(2):

        @pl.when(core == here)
        def _(here=here):
            lanes = slice(here * HALF, (here + 1) * HALF)
            x_half_ref[here] = x_ref[:, lanes]
            x_half_ref[1 - here] = pair_ref[:, lanes]
            c_half_ref[here] = c_ref[:, lanes]
            c_half_ref[1 - here] = pair_ref[:, 256:384]

    turned_ref[core] = x_ref[...].T
    turned_ref[mate] = pair_ref[:, 0:256].T
    for brick in range(2):
        parts[brick] = x_half_ref[brick].astype(f32)
        for k, *shifts in OFFSETS:
            target = jnp.where(core == brick, links_ref[k], mate_links_ref[k])

            @pl.when(target >= 0)
            def _(brick=brick, target=target, shifts=tuple(shifts)):
                rows = region(parts.at[brick], shifts)
                slots[target // 2 - chip + 4, 2 * brick + lax.rem(target, 2), 0 : rows.shape[0], :] = rows.astype(bf16)

    copies = [
        pltpu.make_async_copy(slots.at[hop + 4], out, sems.at[n])
        for n, (hop, out) in enumerate(zip(HOPS + (0,), outs))
    ]
    for copy in copies:
        copy.start()
    for copy in copies:
        copy.wait()


def prepare(links, mate_links, x, c, pair):
    half = jax.ShapeDtypeStruct((2, 512, HALF), bf16)
    got = pl.pallas_call(
        prepare_kernel,
        out_shape=tuple(jax.ShapeDtypeStruct((4, 64, HALF), bf16) for hop in HOPS + (0,))
        + (jax.ShapeDtypeStruct((2, 256, 512), bf16), half, half),
        in_specs=[smem(), smem(), vmem(), vmem(), vmem()],
        out_specs=(anywhere(),) * 5 + (vmem(),) * 3,
        scratch_shapes=[
            pltpu.VMEM((2, 512, HALF), f32),
            pltpu.VMEM((9, 4, 64, HALF), bf16),
            pltpu.SemaphoreType.DMA((5,)),
        ],
        compiler_params=params(LP),
        cost_estimate=cost(2.5),
    )(links, mate_links, x, c, pair)
    return got[:5], *got[5:]


def target_plane(shift):
    return 9 if shift > 0 else 0


def scaling(peak):
    code = jnp.ceil(jnp.log2(jnp.maximum(peak, 2.0**-110)) * 256.0) + 1.0
    return LEVELS * jnp.exp2(code * (-1.0 / 256.0)), code


def fixed(values):
    return jnp.round(values).astype(i32).astype(i16)


def plain(coded):
    return coded.astype(i32).astype(f32)


def step_of(code):
    return jnp.exp2(code * (1.0 / 256.0)) * (1.0 / LEVELS)


def fill(brick, links, fetch, own_rows, plane, low, high, shifted_low, shifted_high, padded):
    plane[...] = jnp.zeros_like(plane)
    low[...] = jnp.zeros_like(low)
    high[...] = jnp.zeros_like(high)
    for x in range(8):
        plane[pl.ds((x + 1) * 80 + 8, 64), :] = own_rows(x * 64)
    for k, dx, dy, dz in OFFSETS:
        source = links[k]

        @pl.when(source >= 0)
        def _(source=source, k=k, dx=dx, dy=dy, dz=dz):
            at_x, at_y = target_plane(dx), target_plane(dy)
            face = (dx != 0) + (dy != 0) + (dz != 0) == 1
            got = fetch(source, brick, k, 64 if face else 16).astype(f32)
            if dz == 0:
                if dy == 0:
                    plane[pl.ds(at_x * 80 + 8, 64), :] = got
                elif dx == 0:
                    for x in range(8):
                        plane[pl.ds((x + 1) * 80 + at_y * 8, 8), :] = got[x * 8 : x * 8 + 8]
                else:
                    plane[pl.ds(at_x * 80 + at_y * 8, 8), :] = got[0:8]
            else:
                rim = low if dz < 0 else high
                if dx == 0 and dy == 0:
                    for x in range(8):
                        rim[pl.ds((x + 1) * 10 + 1, 8), :] = got[x * 8 : x * 8 + 8]
                elif dy == 0:
                    rim[pl.ds(at_x * 10 + 1, 8), :] = got[0:8]
                elif dx == 0:
                    rim[pl.ds(10 + at_y, 8, stride=10), :] = got[0:8]
                else:
                    rim[pl.ds(at_x * 10 + at_y, 1), :] = got[0:1]

    shifted_low[pl.ds(1, 800), :] = plane[pl.ds(0, 800), :]
    shifted_low[pl.ds(0, 104, stride=8), :] = low[...]
    shifted_high[pl.ds(0, 800), :] = plane[pl.ds(1, 800), :]
    shifted_high[pl.ds(7, 104, stride=8), :] = high[...]
    for j in range(3):
        for l, source in enumerate((shifted_low, plane, shifted_high)):
            at = (3 * j + l) * HALF
            for x in range(10):
                padded[brick, x * 64 : x * 64 + 64, at : at + HALF] = source[pl.ds(x * 80 + j * 8, 64), :].astype(bf16)


def fill_both(core, links_ref, mate_links_ref, half_ref, fetch, scratch):
    for brick in range(2):

        def rows(first, brick=brick):
            return half_ref[brick, pl.ds(first, 64), :].astype(f32)

        fill(brick, [jnp.where(core == brick, links_ref[k], mate_links_ref[k]) for k in range(27)], fetch, rows, *scratch)


def by_distance(halo_ref, chip):
    return lambda source, brick, k, count: halo_ref[source // 2 - chip + 4, 2 * lax.rem(source, 2) + brick, 0:count, :]


FILL_SCRATCH = [
    pltpu.VMEM((832, HALF), f32),
    pltpu.VMEM((104, HALF), f32),
    pltpu.VMEM((104, HALF), f32),
    pltpu.VMEM((832, HALF), f32),
    pltpu.VMEM((832, HALF), f32),
    pltpu.VMEM((2, 640, 9 * HALF), bf16),
]


def by_device(halo_ref):
    return lambda source, brick, k, count: halo_ref[source, brick, 0:count, :]


def kernel_grad_kernel(links_ref, mate_links_ref, c_half_ref, turned_ref, halo_ref, terms_ref, grads, coded, sems, *scratch):
    core = lax.rem(position()[0], 2)
    padded = scratch[-1]
    fill_both(core, links_ref, mate_links_ref, c_half_ref, by_device(halo_ref), scratch)
    for i in range(3):
        window = slice(i * 64, i * 64 + 512)
        term = jnp.dot(turned_ref[0], padded[0, window, :], preferred_element_type=f32)
        term += jnp.dot(turned_ref[1], padded[1, window, :], preferred_element_type=f32)
        for jl in range(9):
            grads[26 - (9 * i + jl)] = term[:, jl * HALF : (jl + 1) * HALF]
    copies = []
    for q in range(CHIPS):
        def rows(k, q=q):
            return jnp.concatenate([grads[k, pl.ds(at + q * 8, 8), :] for at in (0, 128)], axis=0)

        peak = jnp.abs(rows(0))
        for k in range(1, 27):
            peak = jnp.maximum(peak, jnp.abs(rows(k)))
        factor, code = scaling(jnp.max(peak, axis=0, keepdims=True))
        for k in range(27):
            coded[q, k * 16 : k * 16 + 16, :] = fixed(rows(k) * factor)
        coded[q, 432:448, :] = fixed(jnp.broadcast_to(code, (16, HALF)))
        copies.append(pltpu.make_async_copy(coded.at[q], terms_ref.at[q], sems.at[q]))
        copies[-1].start()
    for copy in copies:
        copy.wait()


def kernel_grad(links, mate_links, c_half, turned, halo):
    return pl.pallas_call(
        kernel_grad_kernel,
        out_shape=jax.ShapeDtypeStruct((CHIPS, 448, HALF), i16),
        in_specs=[smem(), smem(), vmem(), vmem(), vmem()],
        out_specs=anywhere(),
        scratch_shapes=[
            pltpu.VMEM((27, 256, HALF), f32),
            pltpu.VMEM((CHIPS, 448, HALF), i16),
            pltpu.SemaphoreType.DMA((CHIPS,)),
        ]
        + FILL_SCRATCH,
        compiler_params=params(LG),
        cost_estimate=cost(6.0),
    )(links, mate_links, c_half, turned, halo)


def taps_kernel(turned, links_ref, mate_links_ref, half_ref, weight_ref, halo_ref, *rest):
    own = position()[0]
    core = lax.rem(own, 2)
    start = pl.multiple_of(core * HALF, HALF)
    if turned:
        _, out_ref, mate_out_ref, taps, sems, *scratch = rest
        fetch = by_device(halo_ref)
        halo_copies = []
        copies = [
            pltpu.make_async_copy(
                weight_ref.at[26 - k, :, pl.ds(start, HALF)], taps.at[:, pl.ds(k * HALF, HALF)], sems.at[k]
            )
            for k in range(27)
        ]
    else:
        halos, (out_ref, mate_out_ref, taps, sems, slots, far_sems, *scratch) = rest[:5], rest[5:]
        chip = own // 2
        fetch = by_distance(slots, chip)
        halo_copies = [
            pltpu.make_async_copy(halo, slots.at[4 - hop], sems.at[1 + n])
            for n, (hop, halo) in enumerate(zip(HOPS + (0,), halos))
        ]
        for hop in (-4, -3, 3, 4):
            source = jnp.clip(chip + hop, 0, CHIPS - 1)
            for side_by in range(4):
                halo_copies.append(
                    pltpu.make_async_copy(
                        halo_ref.at[2 * source + side_by // 2, side_by % 2, pl.ds(16, 16), :],
                        slots.at[4 + hop, side_by, pl.ds(0, 16), :],
                        far_sems.at[4 + hop, side_by],
                    )
                )
        copies = [pltpu.make_async_copy(weight_ref.at[:, pl.ds(start, HALF), :], taps, sems.at[0])]
    padded = scratch[-1]
    for copy in halo_copies + copies:
        copy.start()
    for copy in halo_copies:
        copy.wait()
    fill_both(core, links_ref, mate_links_ref, half_ref, fetch, scratch)
    for copy in copies:
        copy.wait()
    for to_mate, out in ((0, out_ref), (1, mate_out_ref)):
        brick = lax.rem(core + to_mate, 2)
        total = jnp.zeros((512, 256), f32)
        for i in range(3):
            block = padded[brick, i * 64 : i * 64 + 512, :]
            if turned:
                now = taps[:, i * 9 * HALF : (i + 1) * 9 * HALF]
                total += lax.dot_general(block, now, (((1,), (1,)), ((), ())), preferred_element_type=f32)
            else:
                now = taps[9 * i : 9 * i + 9].reshape(9 * HALF, 256)
                total += jnp.dot(block, now, preferred_element_type=f32)
        out[...] = total


def taps_product(turned, links, mate_links, half, weight, halo, *rest):
    taps = pltpu.VMEM((256, 27 * HALF) if turned else (27, HALF, 256), bf16)
    slots = [] if turned else [pltpu.VMEM((9, 4, 64, HALF), bf16), pltpu.SemaphoreType.DMA((9, 4))]
    return pl.pallas_call(
        functools.partial(taps_kernel, turned),
        out_shape=(jax.ShapeDtypeStruct((512, 256), f32),) * 2,
        in_specs=[smem(), smem(), vmem(), hbm(), vmem() if turned else hbm()] + [anywhere()] * len(rest),
        out_specs=(vmem(), vmem()),
        scratch_shapes=[taps, pltpu.SemaphoreType.DMA((28,))] + slots + FILL_SCRATCH,
        compiler_params=params(56),
        cost_estimate=cost(6.0),
    )(links, mate_links, half, weight, halo, *rest)


def first_unit(chip, scene):
    return lax.rem(chip - 12 * scene + 96, 16)


def coded_block(values):
    factor, code = scaling(jnp.max(jnp.abs(values), axis=0, keepdims=True))
    return fixed(jnp.concatenate([values * factor, jnp.broadcast_to(code, (8, HALF))], axis=0))


def plain_block(coded):
    values = plain(coded)
    return values[0:56] * step_of(values[56:57])


def scene_kernel(got_ref, out_ref, total):
    chip = position()[0] // 2
    steps = [step_of(plain(got_ref[source, 432:448, :])) for source in range(CHIPS)]
    for k in range(27):
        sums = jnp.zeros((16, HALF), f32)
        for source in range(CHIPS):
            sums += plain(got_ref[source, k * 16 : k * 16 + 16, :]) * steps[source]
        total[2 * k] = sums[0:8]
        total[2 * k + 1] = sums[8:16]
    total[54] = jnp.zeros((8, HALF), f32)
    for scene in range(SCENES):
        first = (108 * scene + first_unit(chip, scene) - chip) // 16
        units = [total[jnp.minimum(first + t, 54)] for t in range(7)]
        out_ref[scene] = coded_block(jnp.concatenate(units, axis=0))


def scene_sum(got):
    return pl.pallas_call(
        scene_kernel,
        out_shape=jax.ShapeDtypeStruct((SCENES, 64, HALF), i16),
        in_specs=[vmem()],
        out_specs=vmem(),
        scratch_shapes=[pltpu.VMEM((55, 8, HALF), f32)],
        compiler_params=params(LS),
        cost_estimate=cost(2.5),
    )(got)


def whole_kernel(scale, got_ref, out_ref):
    total = plain_block(got_ref[0])
    for scene in range(1, SCENES):
        total += plain_block(got_ref[scene])
    block = coded_block(total * scale)
    for target in range(SPACE):
        out_ref[target] = block


def whole_sum(scale, got):
    return pl.pallas_call(
        functools.partial(whole_kernel, scale),
        out_shape=jax.ShapeDtypeStruct((SPACE, 64, HALF), i16),
        in_specs=[vmem()],
        out_specs=vmem(),
        compiler_params=params(LW),
        cost_estimate=cost(1.5),
    )(got)


def place_kernel(got_ref, out_ref, whole, sems):
    scene = position()[1]
    outs = [
        pltpu.make_async_copy(whole.at[pl.ds(t * 128, size), :], out_ref.at[pl.ds(t * 128, size), :], sems.at[t])
        for t, size in enumerate((128,) * 6 + (96,))
    ]
    steps = [step_of(plain(got_ref[source, 48:64, :])[8:9]) for source in range(SPACE)]
    for t in range(0, 7, 2):
        for chip in range(CHIPS):
            rest = first_unit(chip, scene)
            for half in range(2):
                source = 2 * chip + half
                lanes = slice(half * HALF, (half + 1) * HALF)
                values = plain(got_ref[source, t * 8 : t * 8 + 16, :]) * steps[source]
                for now in range(t, min(t + 2, 7)):
                    at = pl.multiple_of((16 * now + rest) * 8, 8)
                    whole[pl.ds(at, 8), lanes] = values[(now - t) * 8 : (now - t + 1) * 8]
        for now in range(t, min(t + 2, 7)):
            outs[now].start()
    for copy in outs:
        copy.wait()


def place(got):
    return pl.pallas_call(
        place_kernel,
        out_shape=jax.ShapeDtypeStruct((864, 256), f32),
        in_specs=[vmem()],
        out_specs=hbm(),
        scratch_shapes=[pltpu.VMEM((896, 256), f32), pltpu.SemaphoreType.DMA((7,))],
        compiler_params=params(8),
    )(got)


def body(features, grad_out, weight, neighbours):
    x = features[0, 0]
    c = grad_out[0, 0]
    links = neighbours[0, 0]
    mates = [(i, i ^ 1) for i in range(SPACE)]
    same_core = [[2 * q + core for q in range(CHIPS)] for core in range(2)]
    grad_scale = 1.0 / math.sqrt(SCENES * SPACE * 512)

    mate_links = lax.ppermute(links, "space", mates)
    outgoing_c = pack(links, x, c)
    halo_c = lax.all_to_all(outgoing_c, "space", 0, 0, tiled=True)
    pair = lax.ppermute(pair_rows(x, c, outgoing_c), "space", mates)
    outgoing_x, turned, x_half, c_half = prepare(links, mate_links, x, c, pair)
    halo_x = [
        lax.ppermute(rows, "space", [(i, i + 2 * hop) for i in range(SPACE) if 0 <= i + 2 * hop < SPACE])
        for hop, rows in zip(HOPS, outgoing_x)
    ]
    terms = kernel_grad(links, mate_links, c_half, turned, halo_c)
    got_terms = lax.all_to_all(terms, "space", 0, 0, tiled=True, axis_index_groups=same_core)
    grad_in, mate_grad_in = taps_product(True, links, mate_links, c_half, weight, halo_c, terms)
    got_terms, grad_in, mate_grad_in = lax.optimization_barrier((got_terms, grad_in, mate_grad_in))
    scene_terms = lax.all_to_all(scene_sum(got_terms), "dp", 0, 0, tiled=True)
    conv_out, mate_conv_out = taps_product(False, links, mate_links, x_half, weight, halo_c, *halo_x, outgoing_x[4])
    scene_terms, conv_out, mate_conv_out = lax.optimization_barrier((scene_terms, conv_out, mate_conv_out))
    whole = lax.all_to_all(whole_sum(grad_scale, scene_terms), "space", 0, 0, tiled=True)
    grad_in = (grad_in + lax.ppermute(mate_grad_in, "space", mates)).astype(bf16)
    conv_out = (conv_out + lax.ppermute(mate_conv_out, "space", mates)).astype(bf16)
    return conv_out[None, None], grad_in[None, None], place(whole)


def solution(mesh):
    placed = (
        P("dp", "space", None, None),
        P("dp", "space", None, None),
        P(),
        P("dp", "space", None),
    )
    return jax.shard_map(
        body,
        mesh=mesh,
        in_specs=placed,
        out_specs=(P("dp", "space", None, None), P("dp", "space", None, None), P("dp", None)),
        check_vma=False,
    )
```

```python
import functools
import math

import jax
import jax.numpy as jnp
from jax import lax
from jax.experimental import pallas as pl
from jax.experimental.pallas import tpu as pltpu
from jax.sharding import PartitionSpec as P

f32 = jnp.float32
bf16 = jnp.bfloat16
i16 = jnp.int16
i32 = jnp.int32

SPACE = 32
LG, LS, LW, LP, LQ = 51, 50, 50, 51, 51

SCENES = 8
CHIPS = 16
HALF = 128
LEVELS = 32766.0

ROWS = (256, 192, 64, 16)
FIRST = (0, 256, 448, 512)
BELOW = 528
HERE = 1056

OFFSETS = [(k, k // 9 - 1, k // 3 % 3 - 1, k % 3 - 1) for k in range(27) if k != 13]


def position():
    return lax.axis_index("space"), lax.axis_index("dp")


def params(mib):
    return pltpu.CompilerParams(vmem_limit_bytes=mib << 20)


def cost(us):
    return pl.CostEstimate(flops=int(us * 1e9), bytes_accessed=1 << 20, transcendentals=0)


def vmem():
    return pl.BlockSpec(memory_space=pltpu.VMEM)


def smem():
    return pl.BlockSpec(memory_space=pltpu.SMEM)


def hbm():
    return pl.BlockSpec(memory_space=pltpu.HBM)


def anywhere():
    return pl.BlockSpec(memory_space=pl.ANY)


def side(shift):
    return 7 if shift > 0 else 0


def region(ref, shifts):
    dx, dy, dz = shifts
    kinds = (dx != 0, dy != 0, dz != 0)
    if kinds == (True, False, False):
        return ref[pl.ds(side(dx) * 64, 64), :]
    if kinds == (False, True, False):
        return jnp.concatenate([ref[pl.ds(x * 64 + side(dy) * 8, 8), :] for x in range(8)], axis=0)
    if kinds == (False, False, True):
        return ref[pl.ds(side(dz), 64, stride=8), :]
    if kinds == (True, True, False):
        rows = ref[pl.ds(side(dx) * 64 + side(dy) * 8, 8), :]
    elif kinds == (True, False, True):
        rows = ref[pl.ds(side(dx) * 64 + side(dz), 8, stride=8), :]
    elif kinds == (False, True, True):
        rows = ref[pl.ds(side(dy) * 8 + side(dz), 8, stride=64), :]
    else:
        row = ref[pl.ds(side(dx) * 64 + side(dy) * 8 + side(dz), 1), :]
        rows = jnp.broadcast_to(row, (8, HALF))
    return jnp.concatenate([rows, rows], axis=0)


def is_face(shifts):
    return sum(map(abs, shifts)) == 1


def reach(shifts):
    return abs(shifts[0] + 2 * shifts[1] + 4 * shifts[2])


def place_in_slots(distance, shifts, source, target):
    if distance <= 1:
        return 64 * (2 * source + target)
    if distance == 2:
        return 96 * source + (0 if is_face(shifts) else 64 + 16 * target)
    return 16 * (2 * source + target) if distance == 3 else 0


def pack_kernel(links_ref, mate_links_ref, own_ref, mate_x_ref, mate_c_ref, *rest):
    outs, parts = rest[:4], rest[4]
    own = position()[0]
    core = lax.rem(own, 2)
    chip = own // 2
    for group in range(4):
        lanes = slice(group * HALF, (group + 1) * HALF)
        parts[core, group] = own_ref[:, lanes].astype(f32)
        mate_ref, at = (mate_x_ref, lanes) if group < 2 else (mate_c_ref, slice(lanes.start - 256, lanes.stop - 256))
        parts[1 - core, group] = mate_ref[:, at].astype(f32)
    for brick in range(2):
        for k, *shifts in OFFSETS:
            target = jnp.where(core == brick, links_ref[k], mate_links_ref[k])
            distance = (target // 2 - chip) * (1 - 2 * core)
            to = lax.rem(target, 2)

            @pl.when((target >= 0) & (distance > 0))
            def _(brick=brick, distance=distance, to=to, shifts=tuple(shifts)):
                for step in range(1, 5):
                    if reach(shifts) >= 2 * step - 1:

                        @pl.when(distance == step)
                        def _(step=step):
                            at = pl.multiple_of(place_in_slots(step, shifts, brick, to), 16)
                            for group in range(4):
                                rows = region(parts.at[brick, group], shifts)
                                lanes = slice(group * HALF, (group + 1) * HALF)
                                outs[step - 1][pl.ds(at, rows.shape[0]), lanes] = rows.astype(bf16)


def pack(links, mate_links, own, mate_x, mate_c):
    return pl.pallas_call(
        pack_kernel,
        out_shape=tuple(jax.ShapeDtypeStruct((rows, 512), bf16) for rows in ROWS),
        in_specs=[smem(), smem()] + [vmem()] * 3,
        out_specs=(vmem(),) * 4,
        scratch_shapes=[pltpu.VMEM((2, 4, 512, HALF), f32)],
        compiler_params=params(LQ),
        cost_estimate=cost(2.5),
    )(links, mate_links, own, mate_x, mate_c)


def stage_kernel(
    links_ref, mate_links_ref, own_ref, mate_x_ref, mate_c_ref, _, here_ref, turned_ref, x_half_ref, c_half_ref, parts
):
    own = position()[0]
    core = lax.rem(own, 2)
    for here in range(2):

        @pl.when(core == here)
        def _(here=here):
            lanes = slice(here * HALF, (here + 1) * HALF)
            x_half_ref[here] = own_ref[:, lanes]
            x_half_ref[1 - here] = mate_x_ref[:, lanes]
            c_half_ref[here] = own_ref[:, 256 + here * HALF : 256 + (here + 1) * HALF]
            c_half_ref[1 - here] = mate_c_ref[:, lanes]

    for brick in range(2):
        parts[brick, 0] = x_half_ref[brick].astype(f32)
        parts[brick, 1] = c_half_ref[brick].astype(f32)
        for k, *shifts in OFFSETS:
            target = jnp.where(core == brick, links_ref[k], mate_links_ref[k])

            @pl.when((target >= 0) & (target // 2 == own // 2))
            def _(brick=brick, target=target, shifts=tuple(shifts)):
                at = pl.multiple_of(place_in_slots(0, shifts, brick, lax.rem(target, 2)), 16)
                for tensor in range(2):
                    rows = region(parts.at[brick, tensor], shifts)
                    here_ref[pl.ds(at, rows.shape[0]), tensor * HALF : (tensor + 1) * HALF] = rows.astype(bf16)

    turned_ref[core] = own_ref[:, 0:256].T
    turned_ref[1 - core] = mate_x_ref[...].T


def stage(links, mate_links, own, mate_x, mate_c, after):
    half = jax.ShapeDtypeStruct((2, 512, HALF), bf16)
    return pl.pallas_call(
        stage_kernel,
        out_shape=(
            jax.ShapeDtypeStruct((256, 256), bf16),
            jax.ShapeDtypeStruct((2, 256, 512), bf16),
            half,
            half,
        ),
        in_specs=[smem(), smem()] + [vmem()] * 3 + [anywhere()],
        out_specs=(vmem(),) * 4,
        scratch_shapes=[pltpu.VMEM((2, 2, 512, HALF), f32)],
        compiler_params=params(LP),
        cost_estimate=cost(1.5),
    )(links, mate_links, own, mate_x, mate_c, after)


def target_plane(shift):
    return 9 if shift > 0 else 0


def scaling(peak):
    code = jnp.ceil(jnp.log2(jnp.maximum(peak, 2.0**-110)) * 256.0) + 1.0
    return LEVELS * jnp.exp2(code * (-1.0 / 256.0)), code


def fixed(values):
    return jnp.round(values).astype(i32).astype(i16)


def plain(coded):
    return coded.astype(i32).astype(f32)


def step_of(code):
    return jnp.exp2(code * (1.0 / 256.0)) * (1.0 / LEVELS)


def fill(brick, links, fetch, own_rows, plane, low, high, shifted_low, shifted_high, padded):
    plane[...] = jnp.zeros_like(plane)
    low[...] = jnp.zeros_like(low)
    high[...] = jnp.zeros_like(high)
    for x in range(8):
        plane[pl.ds((x + 1) * 80 + 8, 64), :] = own_rows(x * 64)
    for k, dx, dy, dz in OFFSETS:
        source = links[k]

        @pl.when(source >= 0)
        def _(source=source, dx=dx, dy=dy, dz=dz):
            at_x, at_y = target_plane(dx), target_plane(dy)
            face = (dx != 0) + (dy != 0) + (dz != 0) == 1
            got = fetch(source, brick, (dx, dy, dz), 64 if face else 16).astype(f32)
            if dz == 0:
                if dy == 0:
                    plane[pl.ds(at_x * 80 + 8, 64), :] = got
                elif dx == 0:
                    for x in range(8):
                        plane[pl.ds((x + 1) * 80 + at_y * 8, 8), :] = got[x * 8 : x * 8 + 8]
                else:
                    plane[pl.ds(at_x * 80 + at_y * 8, 8), :] = got[0:8]
            else:
                rim = low if dz < 0 else high
                if dx == 0 and dy == 0:
                    for x in range(8):
                        rim[pl.ds((x + 1) * 10 + 1, 8), :] = got[x * 8 : x * 8 + 8]
                elif dy == 0:
                    rim[pl.ds(at_x * 10 + 1, 8), :] = got[0:8]
                elif dx == 0:
                    rim[pl.ds(10 + at_y, 8, stride=10), :] = got[0:8]
                else:
                    rim[pl.ds(at_x * 10 + at_y, 1), :] = got[0:1]

    shifted_low[pl.ds(1, 800), :] = plane[pl.ds(0, 800), :]
    shifted_low[pl.ds(0, 104, stride=8), :] = low[...]
    shifted_high[pl.ds(0, 800), :] = plane[pl.ds(1, 800), :]
    shifted_high[pl.ds(7, 104, stride=8), :] = high[...]
    for j in range(3):
        for l, source in enumerate((shifted_low, plane, shifted_high)):
            at = (3 * j + l) * HALF
            for x in range(10):
                padded[brick, x * 64 : x * 64 + 64, at : at + HALF] = source[pl.ds(x * 80 + j * 8, 64), :].astype(bf16)


def fill_both(core, links_ref, mate_links_ref, half_ref, fetch, scratch):
    for brick in range(2):

        def rows(first, brick=brick):
            return half_ref[brick, pl.ds(first, 64), :].astype(f32)

        fill(brick, [jnp.where(core == brick, links_ref[k], mate_links_ref[k]) for k in range(27)], fetch, rows, *scratch)


def take_halos(tensor, own, halos, slots, sems):
    core = lax.rem(own, 2)
    chip = own // 2
    lanes = pl.ds(pl.multiple_of(2 * tensor * HALF + core * HALF, HALF), HALF)
    copies = []
    for n, (halo, rows, first) in enumerate(zip(halos[:8], ROWS * 2, FIRST * 2)):
        side = (1 - core) if n < 4 else core
        at = pl.multiple_of(side * BELOW + first, 16)
        copies.append(pltpu.make_async_copy(halo.at[:, lanes], slots.at[pl.ds(at, rows), :], sems.at[n]))
    copies.append(
        pltpu.make_async_copy(halos[8].at[:, pl.ds(tensor * HALF, HALF)], slots.at[pl.ds(HERE, 256), :], sems.at[8])
    )

    def fetch(source, brick, shifts, count):
        apart = source // 2 - chip
        distance = jnp.abs(apart)
        source = lax.rem(source, 2)
        at = HERE + place_in_slots(0, shifts, source, brick)
        for step in range(1, 5):
            if reach(shifts) >= 2 * step - 1:
                there = FIRST[step - 1] + place_in_slots(step, shifts, source, brick)
                at = jnp.where(distance == step, there + jnp.where(apart < 0, BELOW, 0), at)
        return slots[pl.ds(pl.multiple_of(at, 16), count), :]

    return copies, fetch


HALO_SCRATCH = [pltpu.VMEM((HERE + 256, HALF), bf16), pltpu.SemaphoreType.DMA((9,))]
FILL_SCRATCH = [
    pltpu.VMEM((832, HALF), f32),
    pltpu.VMEM((104, HALF), f32),
    pltpu.VMEM((104, HALF), f32),
    pltpu.VMEM((832, HALF), f32),
    pltpu.VMEM((832, HALF), f32),
    pltpu.VMEM((2, 640, 9 * HALF), bf16),
]


def kernel_grad_kernel(links_ref, mate_links_ref, c_half_ref, turned_ref, *rest):
    halos, (terms_ref, grads, coded, sems, slots, halo_sems, *scratch) = rest[:9], rest[9:]
    own = position()[0]
    padded = scratch[-1]
    halo_copies, fetch = take_halos(1, own, halos, slots, halo_sems)
    for copy in halo_copies:
        copy.start()
    for copy in halo_copies:
        copy.wait()
    fill_both(lax.rem(own, 2), links_ref, mate_links_ref, c_half_ref, fetch, scratch)
    for i in range(3):
        window = slice(i * 64, i * 64 + 512)
        term = jnp.dot(turned_ref[0], padded[0, window, :], preferred_element_type=f32)
        term += jnp.dot(turned_ref[1], padded[1, window, :], preferred_element_type=f32)
        for jl in range(9):
            grads[26 - (9 * i + jl)] = term[:, jl * HALF : (jl + 1) * HALF]
    copies = []
    for q in range(CHIPS):
        def rows(k, q=q):
            return jnp.concatenate([grads[k, pl.ds(at + q * 8, 8), :] for at in (0, 128)], axis=0)

        peak = jnp.abs(rows(0))
        for k in range(1, 27):
            peak = jnp.maximum(peak, jnp.abs(rows(k)))
        factor, code = scaling(jnp.max(peak, axis=0, keepdims=True))
        for k in range(27):
            coded[q, k * 16 : k * 16 + 16, :] = fixed(rows(k) * factor)
        coded[q, 432:448, :] = fixed(jnp.broadcast_to(code, (16, HALF)))
        copies.append(pltpu.make_async_copy(coded.at[q], terms_ref.at[q], sems.at[q]))
        copies[-1].start()
    for copy in copies:
        copy.wait()


def kernel_grad(links, mate_links, c_half, turned, halos):
    return pl.pallas_call(
        kernel_grad_kernel,
        out_shape=jax.ShapeDtypeStruct((CHIPS, 448, HALF), i16),
        in_specs=[smem(), smem(), vmem(), vmem()] + [anywhere()] * 9,
        out_specs=anywhere(),
        scratch_shapes=[
            pltpu.VMEM((27, 256, HALF), f32),
            pltpu.VMEM((CHIPS, 448, HALF), i16),
            pltpu.SemaphoreType.DMA((CHIPS,)),
        ]
        + HALO_SCRATCH
        + FILL_SCRATCH,
        compiler_params=params(LG),
        cost_estimate=cost(6.0),
    )(links, mate_links, c_half, turned, *halos)


def taps_kernel(turned, links_ref, mate_links_ref, half_ref, weight_ref, *rest):
    halos, (_, out_ref, mate_out_ref, taps, sems, slots, halo_sems, *scratch) = rest[:9], rest[9:]
    own = position()[0]
    core = lax.rem(own, 2)
    start = pl.multiple_of(core * HALF, HALF)
    halo_copies, fetch = take_halos(1 if turned else 0, own, halos, slots, halo_sems)
    if turned:
        copies = [
            pltpu.make_async_copy(
                weight_ref.at[26 - k, :, pl.ds(start, HALF)], taps.at[:, pl.ds(k * HALF, HALF)], sems.at[k]
            )
            for k in range(27)
        ]
    else:
        copies = [pltpu.make_async_copy(weight_ref.at[:, pl.ds(start, HALF), :], taps, sems.at[0])]
    padded = scratch[-1]
    for copy in halo_copies + copies:
        copy.start()
    for copy in halo_copies:
        copy.wait()
    fill_both(core, links_ref, mate_links_ref, half_ref, fetch, scratch)
    for copy in copies:
        copy.wait()
    for to_mate, out in ((0, out_ref), (1, mate_out_ref)):
        brick = lax.rem(core + to_mate, 2)
        total = jnp.zeros((512, 256), f32)
        for i in range(3):
            block = padded[brick, i * 64 : i * 64 + 512, :]
            if turned:
                now = taps[:, i * 9 * HALF : (i + 1) * 9 * HALF]
                total += lax.dot_general(block, now, (((1,), (1,)), ((), ())), preferred_element_type=f32)
            else:
                now = taps[9 * i : 9 * i + 9].reshape(9 * HALF, 256)
                total += jnp.dot(block, now, preferred_element_type=f32)
        out[...] = total


def taps_product(turned, links, mate_links, half, weight, halos, after):
    taps = pltpu.VMEM((256, 27 * HALF) if turned else (27, HALF, 256), bf16)
    return pl.pallas_call(
        functools.partial(taps_kernel, turned),
        out_shape=(jax.ShapeDtypeStruct((512, 256), f32),) * 2,
        in_specs=[smem(), smem(), vmem(), hbm()] + [anywhere()] * 10,
        out_specs=(vmem(), vmem()),
        scratch_shapes=[taps, pltpu.SemaphoreType.DMA((27,))] + HALO_SCRATCH + FILL_SCRATCH,
        compiler_params=params(56),
        cost_estimate=cost(6.0),
    )(links, mate_links, half, weight, *halos, after)


def first_unit(chip, scene):
    return lax.rem(chip - 12 * scene + 96, 16)


def coded_block(values):
    factor, code = scaling(jnp.max(jnp.abs(values), axis=0, keepdims=True))
    return fixed(jnp.concatenate([values * factor, jnp.broadcast_to(code, (8, HALF))], axis=0))


def plain_block(coded):
    values = plain(coded)
    return values[0:56] * step_of(values[56:57])


def scene_kernel(got_ref, out_ref, total):
    chip = position()[0] // 2
    steps = [step_of(plain(got_ref[source, 432:448, :])) for source in range(CHIPS)]
    for k in range(27):
        sums = jnp.zeros((16, HALF), f32)
        for source in range(CHIPS):
            sums += plain(got_ref[source, k * 16 : k * 16 + 16, :]) * steps[source]
        total[2 * k] = sums[0:8]
        total[2 * k + 1] = sums[8:16]
    total[54] = jnp.zeros((8, HALF), f32)
    for scene in range(SCENES):
        first = (108 * scene + first_unit(chip, scene) - chip) // 16
        units = [total[jnp.minimum(first + t, 54)] for t in range(7)]
        out_ref[scene] = coded_block(jnp.concatenate(units, axis=0))


def scene_sum(got):
    return pl.pallas_call(
        scene_kernel,
        out_shape=jax.ShapeDtypeStruct((SCENES, 64, HALF), i16),
        in_specs=[vmem()],
        out_specs=vmem(),
        scratch_shapes=[pltpu.VMEM((55, 8, HALF), f32)],
        compiler_params=params(LS),
        cost_estimate=cost(2.5),
    )(got)


def whole_kernel(scale, got_ref, out_ref):
    total = plain_block(got_ref[0])
    for scene in range(1, SCENES):
        total += plain_block(got_ref[scene])
    block = coded_block(total * scale)
    for target in range(SPACE):
        out_ref[target] = block


def whole_sum(scale, got):
    return pl.pallas_call(
        functools.partial(whole_kernel, scale),
        out_shape=jax.ShapeDtypeStruct((SPACE, 64, HALF), i16),
        in_specs=[vmem()],
        out_specs=vmem(),
        compiler_params=params(LW),
        cost_estimate=cost(1.5),
    )(got)


def place_kernel(got_ref, out_ref, whole, sems):
    scene = position()[1]
    outs = [
        pltpu.make_async_copy(whole.at[pl.ds(t * 128, size), :], out_ref.at[pl.ds(t * 128, size), :], sems.at[t])
        for t, size in enumerate((128,) * 6 + (96,))
    ]
    steps = [step_of(plain(got_ref[source, 48:64, :])[8:9]) for source in range(SPACE)]
    for t in range(0, 7, 2):
        for chip in range(CHIPS):
            rest = first_unit(chip, scene)
            for half in range(2):
                source = 2 * chip + half
                lanes = slice(half * HALF, (half + 1) * HALF)
                values = plain(got_ref[source, t * 8 : t * 8 + 16, :]) * steps[source]
                for now in range(t, min(t + 2, 7)):
                    at = pl.multiple_of((16 * now + rest) * 8, 8)
                    whole[pl.ds(at, 8), lanes] = values[(now - t) * 8 : (now - t + 1) * 8]
        for now in range(t, min(t + 2, 7)):
            outs[now].start()
    for copy in outs:
        copy.wait()


def place(got):
    return pl.pallas_call(
        place_kernel,
        out_shape=jax.ShapeDtypeStruct((864, 256), f32),
        in_specs=[vmem()],
        out_specs=hbm(),
        scratch_shapes=[pltpu.VMEM((896, 256), f32), pltpu.SemaphoreType.DMA((7,))],
        compiler_params=params(8),
    )(got)


def body(features, grad_out, weight, neighbours):
    x = features[0, 0]
    c = grad_out[0, 0]
    links = jnp.maximum(neighbours[0, 0], -1)
    mates = [(i, i ^ 1) for i in range(SPACE)]
    same_core = [[2 * q + core for q in range(CHIPS)] for core in range(2)]
    grad_scale = 1.0 / math.sqrt(SCENES * SPACE * 512)

    mate_links, mate_x, mate_c = [lax.ppermute(rows, "space", mates) for rows in (links, x, c)]
    own = jnp.concatenate([x, c], axis=1)
    outgoing = pack(links, mate_links, own, mate_x, mate_c)
    halos = []
    for hop, rows in enumerate(outgoing, 1):
        up = [(2 * q, 2 * (q + hop)) for q in range(CHIPS - hop)]
        down = [(2 * (q + hop) + 1, 2 * q + 1) for q in range(CHIPS - hop)]
        halos.append(lax.ppermute(rows, "space", up + down))
    here, turned, x_half, c_half = stage(links, mate_links, own, mate_x, mate_c, outgoing[3])
    *halos, here, turned, x_half, c_half = lax.optimization_barrier((*halos, here, turned, x_half, c_half))
    halos += [lax.ppermute(rows, "space", mates) for rows in halos] + [here]
    terms = kernel_grad(links, mate_links, c_half, turned, halos)
    got_terms = lax.all_to_all(terms, "space", 0, 0, tiled=True, axis_index_groups=same_core)
    grad_in, mate_grad_in = taps_product(True, links, mate_links, c_half, weight, halos, terms)
    conv_out, mate_conv_out = taps_product(False, links, mate_links, x_half, weight, halos, terms)
    got_terms, grad_in, mate_grad_in, conv_out, mate_conv_out = lax.optimization_barrier(
        (got_terms, grad_in, mate_grad_in, conv_out, mate_conv_out)
    )
    scene_terms = lax.all_to_all(scene_sum(got_terms), "dp", 0, 0, tiled=True)
    whole = lax.all_to_all(whole_sum(grad_scale, scene_terms), "space", 0, 0, tiled=True)
    grad_in = (grad_in + lax.ppermute(mate_grad_in, "space", mates)).astype(bf16)
    conv_out = (conv_out + lax.ppermute(mate_conv_out, "space", mates)).astype(bf16)
    return conv_out[None, None], grad_in[None, None], place(whole)


def solution(mesh):
    placed = (
        P("dp", "space", None, None),
        P("dp", "space", None, None),
        P(),
        P("dp", "space", None),
    )
    return jax.shard_map(
        body,
        mesh=mesh,
        in_specs=placed,
        out_specs=(P("dp", "space", None, None), P("dp", "space", None, None), P("dp", None)),
        check_vma=False,
    )
```

```python
import functools
import math

import jax
import jax.numpy as jnp
from jax import lax
from jax.experimental import pallas as pl
from jax.experimental.pallas import tpu as pltpu
from jax.sharding import PartitionSpec as P

f32 = jnp.float32
bf16 = jnp.bfloat16
i16 = jnp.int16
i32 = jnp.int32

SPACE = 32
LG, LS, LW, LP, LQ = 51, 50, 50, 51, 51

SCENES = 8
CHIPS = 16
HALF = 128
LEVELS = 32766.0

ROWS = (256, 192, 64, 16)
FIRST = (0, 256, 448, 512)
BELOW = 528
HERE = 1056

OFFSETS = [(k, k // 9 - 1, k // 3 % 3 - 1, k % 3 - 1) for k in range(27) if k != 13]


def position():
    return lax.axis_index("space"), lax.axis_index("dp")


def params(mib):
    return pltpu.CompilerParams(vmem_limit_bytes=mib << 20)


def cost(us):
    return pl.CostEstimate(flops=int(us * 1e9), bytes_accessed=1 << 20, transcendentals=0)


def vmem():
    return pl.BlockSpec(memory_space=pltpu.VMEM)


def smem():
    return pl.BlockSpec(memory_space=pltpu.SMEM)


def hbm():
    return pl.BlockSpec(memory_space=pltpu.HBM)


def anywhere():
    return pl.BlockSpec(memory_space=pl.ANY)


def side(shift):
    return 7 if shift > 0 else 0


def region(ref, shifts):
    dx, dy, dz = shifts
    kinds = (dx != 0, dy != 0, dz != 0)
    if kinds == (True, False, False):
        return ref[pl.ds(side(dx) * 64, 64), :]
    if kinds == (False, True, False):
        return jnp.concatenate([ref[pl.ds(x * 64 + side(dy) * 8, 8), :] for x in range(8)], axis=0)
    if kinds == (False, False, True):
        return ref[pl.ds(side(dz), 64, stride=8), :]
    if kinds == (True, True, False):
        rows = ref[pl.ds(side(dx) * 64 + side(dy) * 8, 8), :]
    elif kinds == (True, False, True):
        rows = ref[pl.ds(side(dx) * 64 + side(dz), 8, stride=8), :]
    elif kinds == (False, True, True):
        rows = ref[pl.ds(side(dy) * 8 + side(dz), 8, stride=64), :]
    else:
        row = ref[pl.ds(side(dx) * 64 + side(dy) * 8 + side(dz), 1), :]
        rows = jnp.broadcast_to(row, (8, HALF))
    return jnp.concatenate([rows, rows], axis=0)


def is_face(shifts):
    return sum(map(abs, shifts)) == 1


def reach(shifts):
    return abs(shifts[0] + 2 * shifts[1] + 4 * shifts[2])


def place_in_slots(distance, shifts, source, target):
    if distance <= 1:
        return 64 * (2 * source + target)
    if distance == 2:
        return 96 * source + (0 if is_face(shifts) else 64 + 16 * target)
    return 16 * (2 * source + target) if distance == 3 else 0


def pack_kernel(links_ref, mate_links_ref, own_ref, mate_x_ref, mate_c_ref, *rest):
    outs, parts = rest[:4], rest[4]
    own = position()[0]
    core = lax.rem(own, 2)
    chip = own // 2
    for group in range(4):
        lanes = slice(group * HALF, (group + 1) * HALF)
        parts[core, group] = own_ref[:, lanes].astype(f32)
        mate_ref, at = (mate_x_ref, lanes) if group < 2 else (mate_c_ref, slice(lanes.start - 256, lanes.stop - 256))
        parts[1 - core, group] = mate_ref[:, at].astype(f32)
    for brick in range(2):
        for k, *shifts in OFFSETS:
            target = jnp.where(core == brick, links_ref[k], mate_links_ref[k])
            distance = (target // 2 - chip) * (1 - 2 * core)
            to = lax.rem(target, 2)

            @pl.when((target >= 0) & (distance > 0))
            def _(brick=brick, distance=distance, to=to, shifts=tuple(shifts)):
                for step in range(1, 5):
                    if reach(shifts) >= 2 * step - 1:

                        @pl.when(distance == step)
                        def _(step=step):
                            at = pl.multiple_of(place_in_slots(step, shifts, brick, to), 16)
                            for group in range(4):
                                rows = region(parts.at[brick, group], shifts)
                                lanes = slice(group * HALF, (group + 1) * HALF)
                                outs[step - 1][pl.ds(at, rows.shape[0]), lanes] = rows.astype(bf16)


def pack(links, mate_links, own, mate_x, mate_c):
    return pl.pallas_call(
        pack_kernel,
        out_shape=tuple(jax.ShapeDtypeStruct((rows, 512), bf16) for rows in ROWS),
        in_specs=[smem(), smem()] + [vmem()] * 3,
        out_specs=(vmem(),) * 4,
        scratch_shapes=[pltpu.VMEM((2, 4, 512, HALF), f32)],
        compiler_params=params(LQ),
        cost_estimate=cost(2.5),
    )(links, mate_links, own, mate_x, mate_c)


def stage_kernel(
    links_ref, mate_links_ref, own_ref, mate_x_ref, mate_c_ref, _, here_ref, turned_ref, x_half_ref, c_half_ref, parts
):
    own = position()[0]
    core = lax.rem(own, 2)
    for here in range(2):

        @pl.when(core == here)
        def _(here=here):
            lanes = slice(here * HALF, (here + 1) * HALF)
            x_half_ref[here] = own_ref[:, lanes]
            x_half_ref[1 - here] = mate_x_ref[:, lanes]
            c_half_ref[here] = own_ref[:, 256 + here * HALF : 256 + (here + 1) * HALF]
            c_half_ref[1 - here] = mate_c_ref[:, lanes]

    for brick in range(2):
        parts[brick, 0] = x_half_ref[brick].astype(f32)
        parts[brick, 1] = c_half_ref[brick].astype(f32)
        for k, *shifts in OFFSETS:
            target = jnp.where(core == brick, links_ref[k], mate_links_ref[k])

            @pl.when((target >= 0) & (target // 2 == own // 2))
            def _(brick=brick, target=target, shifts=tuple(shifts)):
                at = pl.multiple_of(place_in_slots(0, shifts, brick, lax.rem(target, 2)), 16)
                for tensor in range(2):
                    rows = region(parts.at[brick, tensor], shifts)
                    here_ref[pl.ds(at, rows.shape[0]), tensor * HALF : (tensor + 1) * HALF] = rows.astype(bf16)

    turned_ref[core] = own_ref[:, 0:256].T
    turned_ref[1 - core] = mate_x_ref[...].T


def stage(links, mate_links, own, mate_x, mate_c, after):
    half = jax.ShapeDtypeStruct((2, 512, HALF), bf16)
    return pl.pallas_call(
        stage_kernel,
        out_shape=(
            jax.ShapeDtypeStruct((256, 256), bf16),
            jax.ShapeDtypeStruct((2, 256, 512), bf16),
            half,
            half,
        ),
        in_specs=[smem(), smem()] + [vmem()] * 3 + [anywhere()],
        out_specs=(vmem(),) * 4,
        scratch_shapes=[pltpu.VMEM((2, 2, 512, HALF), f32)],
        compiler_params=params(LP),
        cost_estimate=cost(1.5),
    )(links, mate_links, own, mate_x, mate_c, after)


def target_plane(shift):
    return 9 if shift > 0 else 0


def scaling(peak):
    code = jnp.ceil(jnp.log2(jnp.maximum(peak, 2.0**-110)) * 256.0) + 1.0
    return LEVELS * jnp.exp2(code * (-1.0 / 256.0)), code


def fixed(values):
    return jnp.round(values).astype(i32).astype(i16)


def plain(coded):
    return coded.astype(i32).astype(f32)


def step_of(code):
    return jnp.exp2(code * (1.0 / 256.0)) * (1.0 / LEVELS)


def fill(brick, links, fetch, ready, own_rows, plane, low, high, shifted_low, shifted_high, padded):
    plane[...] = jnp.zeros_like(plane)
    low[...] = jnp.zeros_like(low)
    high[...] = jnp.zeros_like(high)
    for x in range(8):
        plane[pl.ds((x + 1) * 80 + 8, 64), :] = own_rows(x * 64)
    for copy in ready:
        copy.wait()
    for k, dx, dy, dz in OFFSETS:
        source = links[k]

        @pl.when(source >= 0)
        def _(source=source, dx=dx, dy=dy, dz=dz):
            at_x, at_y = target_plane(dx), target_plane(dy)
            face = (dx != 0) + (dy != 0) + (dz != 0) == 1
            got = fetch(source, brick, (dx, dy, dz), 64 if face else 16).astype(f32)
            if dz == 0:
                if dy == 0:
                    plane[pl.ds(at_x * 80 + 8, 64), :] = got
                elif dx == 0:
                    for x in range(8):
                        plane[pl.ds((x + 1) * 80 + at_y * 8, 8), :] = got[x * 8 : x * 8 + 8]
                else:
                    plane[pl.ds(at_x * 80 + at_y * 8, 8), :] = got[0:8]
            else:
                rim = low if dz < 0 else high
                if dx == 0 and dy == 0:
                    for x in range(8):
                        rim[pl.ds((x + 1) * 10 + 1, 8), :] = got[x * 8 : x * 8 + 8]
                elif dy == 0:
                    rim[pl.ds(at_x * 10 + 1, 8), :] = got[0:8]
                elif dx == 0:
                    rim[pl.ds(10 + at_y, 8, stride=10), :] = got[0:8]
                else:
                    rim[pl.ds(at_x * 10 + at_y, 1), :] = got[0:1]

    shifted_low[pl.ds(1, 800), :] = plane[pl.ds(0, 800), :]
    shifted_low[pl.ds(0, 104, stride=8), :] = low[...]
    shifted_high[pl.ds(0, 800), :] = plane[pl.ds(1, 800), :]
    shifted_high[pl.ds(7, 104, stride=8), :] = high[...]
    for j in range(3):
        for l, source in enumerate((shifted_low, plane, shifted_high)):
            at = (3 * j + l) * HALF
            for x in range(10):
                padded[brick, x * 64 : x * 64 + 64, at : at + HALF] = source[pl.ds(x * 80 + j * 8, 64), :].astype(bf16)


def fill_both(core, links_ref, mate_links_ref, half_ref, halo_copies, fetch, scratch):
    for brick in range(2):

        def rows(first, brick=brick):
            return half_ref[brick, pl.ds(first, 64), :].astype(f32)

        links = [jnp.where(core == brick, links_ref[k], mate_links_ref[k]) for k in range(27)]
        fill(brick, links, fetch, halo_copies if brick == 0 else [], rows, *scratch)


def take_halos(tensor, own, halos, slots, sems):
    core = lax.rem(own, 2)
    chip = own // 2
    lanes = pl.ds(pl.multiple_of(2 * tensor * HALF + core * HALF, HALF), HALF)
    copies = []
    for n, (halo, rows, first) in enumerate(zip(halos[:8], ROWS * 2, FIRST * 2)):
        side = (1 - core) if n < 4 else core
        at = pl.multiple_of(side * BELOW + first, 16)
        copies.append(pltpu.make_async_copy(halo.at[:, lanes], slots.at[pl.ds(at, rows), :], sems.at[n]))
    copies.append(
        pltpu.make_async_copy(halos[8].at[:, pl.ds(tensor * HALF, HALF)], slots.at[pl.ds(HERE, 256), :], sems.at[8])
    )

    def fetch(source, brick, shifts, count):
        apart = source // 2 - chip
        distance = jnp.abs(apart)
        source = lax.rem(source, 2)
        at = HERE + place_in_slots(0, shifts, source, brick)
        for step in range(1, 5):
            if reach(shifts) >= 2 * step - 1:
                there = FIRST[step - 1] + place_in_slots(step, shifts, source, brick)
                at = jnp.where(distance == step, there + jnp.where(apart < 0, BELOW, 0), at)
        return slots[pl.ds(pl.multiple_of(at, 16), count), :]

    return copies, fetch


HALO_SCRATCH = [pltpu.VMEM((HERE + 256, HALF), bf16), pltpu.SemaphoreType.DMA((9,))]
FILL_SCRATCH = [
    pltpu.VMEM((832, HALF), f32),
    pltpu.VMEM((104, HALF), f32),
    pltpu.VMEM((104, HALF), f32),
    pltpu.VMEM((832, HALF), f32),
    pltpu.VMEM((832, HALF), f32),
    pltpu.VMEM((2, 640, 9 * HALF), bf16),
]


def kernel_grad_kernel(links_ref, mate_links_ref, c_half_ref, turned_ref, *rest):
    halos, (terms_ref, grads, coded, sems, slots, halo_sems, *scratch) = rest[:9], rest[9:]
    own = position()[0]
    padded = scratch[-1]
    halo_copies, fetch = take_halos(1, own, halos, slots, halo_sems)
    for copy in halo_copies:
        copy.start()
    fill_both(lax.rem(own, 2), links_ref, mate_links_ref, c_half_ref, halo_copies, fetch, scratch)
    for i in range(3):
        window = slice(i * 64, i * 64 + 512)
        term = jnp.dot(turned_ref[0], padded[0, window, :], preferred_element_type=f32)
        term += jnp.dot(turned_ref[1], padded[1, window, :], preferred_element_type=f32)
        for jl in range(9):
            grads[26 - (9 * i + jl)] = term[:, jl * HALF : (jl + 1) * HALF]
    copies = []
    for q in range(CHIPS):
        def rows(k, q=q):
            return jnp.concatenate([grads[k, pl.ds(at + q * 8, 8), :] for at in (0, 128)], axis=0)

        peak = jnp.abs(rows(0))
        for k in range(1, 27):
            peak = jnp.maximum(peak, jnp.abs(rows(k)))
        factor, code = scaling(jnp.max(peak, axis=0, keepdims=True))
        for k in range(27):
            coded[q, k * 16 : k * 16 + 16, :] = fixed(rows(k) * factor)
        coded[q, 432:448, :] = fixed(jnp.broadcast_to(code, (16, HALF)))
        copies.append(pltpu.make_async_copy(coded.at[q], terms_ref.at[q], sems.at[q]))
        copies[-1].start()
    for copy in copies:
        copy.wait()


def kernel_grad(links, mate_links, c_half, turned, halos):
    return pl.pallas_call(
        kernel_grad_kernel,
        out_shape=jax.ShapeDtypeStruct((CHIPS, 448, HALF), i16),
        in_specs=[smem(), smem(), vmem(), vmem()] + [anywhere()] * 9,
        out_specs=anywhere(),
        scratch_shapes=[
            pltpu.VMEM((27, 256, HALF), f32),
            pltpu.VMEM((CHIPS, 448, HALF), i16),
            pltpu.SemaphoreType.DMA((CHIPS,)),
        ]
        + HALO_SCRATCH
        + FILL_SCRATCH,
        compiler_params=params(LG),
        cost_estimate=cost(6.0),
    )(links, mate_links, c_half, turned, *halos)


def taps_kernel(turned, links_ref, mate_links_ref, half_ref, weight_ref, *rest):
    halos, (_, out_ref, mate_out_ref, taps, sems, slots, halo_sems, *scratch) = rest[:9], rest[9:]
    own = position()[0]
    core = lax.rem(own, 2)
    start = pl.multiple_of(core * HALF, HALF)
    halo_copies, fetch = take_halos(1 if turned else 0, own, halos, slots, halo_sems)
    if turned:
        copies = [
            pltpu.make_async_copy(
                weight_ref.at[26 - k, :, pl.ds(start, HALF)], taps.at[:, pl.ds(k * HALF, HALF)], sems.at[k]
            )
            for k in range(27)
        ]
    else:
        copies = [pltpu.make_async_copy(weight_ref.at[:, pl.ds(start, HALF), :], taps, sems.at[0])]
    padded = scratch[-1]
    for copy in halo_copies + copies:
        copy.start()
    fill_both(core, links_ref, mate_links_ref, half_ref, halo_copies, fetch, scratch)
    for copy in copies:
        copy.wait()
    for to_mate, out in ((0, out_ref), (1, mate_out_ref)):
        brick = lax.rem(core + to_mate, 2)
        total = jnp.zeros((512, 256), f32)
        for i in range(3):
            block = padded[brick, i * 64 : i * 64 + 512, :]
            if turned:
                now = taps[:, i * 9 * HALF : (i + 1) * 9 * HALF]
                total += lax.dot_general(block, now, (((1,), (1,)), ((), ())), preferred_element_type=f32)
            else:
                now = taps[9 * i : 9 * i + 9].reshape(9 * HALF, 256)
                total += jnp.dot(block, now, preferred_element_type=f32)
        out[...] = total


def taps_product(turned, links, mate_links, half, weight, halos, after):
    taps = pltpu.VMEM((256, 27 * HALF) if turned else (27, HALF, 256), bf16)
    return pl.pallas_call(
        functools.partial(taps_kernel, turned),
        out_shape=(jax.ShapeDtypeStruct((512, 256), f32),) * 2,
        in_specs=[smem(), smem(), vmem(), hbm()] + [anywhere()] * 10,
        out_specs=(vmem(), vmem()),
        scratch_shapes=[taps, pltpu.SemaphoreType.DMA((27,))] + HALO_SCRATCH + FILL_SCRATCH,
        compiler_params=params(56),
        cost_estimate=cost(6.0),
    )(links, mate_links, half, weight, *halos, after)


def first_unit(chip, scene):
    return lax.rem(chip - 12 * scene + 96, 16)


def coded_block(values):
    factor, code = scaling(jnp.max(jnp.abs(values), axis=0, keepdims=True))
    return fixed(jnp.concatenate([values * factor, jnp.broadcast_to(code, (8, HALF))], axis=0))


def plain_block(coded):
    values = plain(coded)
    return values[0:56] * step_of(values[56:57])


def scene_kernel(got_ref, out_ref, total):
    chip = position()[0] // 2
    steps = [step_of(plain(got_ref[source, 432:448, :])) for source in range(CHIPS)]
    for k in range(27):
        sums = jnp.zeros((16, HALF), f32)
        for source in range(CHIPS):
            sums += plain(got_ref[source, k * 16 : k * 16 + 16, :]) * steps[source]
        total[2 * k] = sums[0:8]
        total[2 * k + 1] = sums[8:16]
    total[54] = jnp.zeros((8, HALF), f32)
    for scene in range(SCENES):
        first = (108 * scene + first_unit(chip, scene) - chip) // 16
        units = [total[jnp.minimum(first + t, 54)] for t in range(7)]
        out_ref[scene] = coded_block(jnp.concatenate(units, axis=0))


def scene_sum(got):
    return pl.pallas_call(
        scene_kernel,
        out_shape=jax.ShapeDtypeStruct((SCENES, 64, HALF), i16),
        in_specs=[vmem()],
        out_specs=vmem(),
        scratch_shapes=[pltpu.VMEM((55, 8, HALF), f32)],
        compiler_params=params(LS),
        cost_estimate=cost(2.5),
    )(got)


def whole_kernel(scale, got_ref, out_ref):
    total = plain_block(got_ref[0])
    for scene in range(1, SCENES):
        total += plain_block(got_ref[scene])
    block = coded_block(total * scale)
    for target in range(CHIPS):
        out_ref[target] = block


def whole_sum(scale, got):
    return pl.pallas_call(
        functools.partial(whole_kernel, scale),
        out_shape=jax.ShapeDtypeStruct((CHIPS, 64, HALF), i16),
        in_specs=[vmem()],
        out_specs=vmem(),
        compiler_params=params(LW),
        cost_estimate=cost(1.5),
    )(got)


def place_kernel(got_ref, mate_ref, out_ref, whole, sems):
    space, scene = position()
    core = lax.rem(space, 2)
    outs = [
        pltpu.make_async_copy(whole.at[pl.ds(t * 128, size), :], out_ref.at[pl.ds(t * 128, size), :], sems.at[t])
        for t, size in enumerate((128,) * 6 + (96,))
    ]
    both = ((got_ref, pl.multiple_of(core * HALF, HALF)), (mate_ref, pl.multiple_of((1 - core) * HALF, HALF)))
    steps = [[step_of(plain(ref[chip, 48:64, :])[8:9]) for chip in range(CHIPS)] for ref, _ in both]
    for t in range(0, 7, 2):
        for chip in range(CHIPS):
            rest = first_unit(chip, scene)
            for n, (ref, at_lane) in enumerate(both):
                values = plain(ref[chip, t * 8 : t * 8 + 16, :]) * steps[n][chip]
                for now in range(t, min(t + 2, 7)):
                    at = pl.multiple_of((16 * now + rest) * 8, 8)
                    whole[pl.ds(at, 8), pl.ds(at_lane, HALF)] = values[(now - t) * 8 : (now - t + 1) * 8]
        for now in range(t, min(t + 2, 7)):
            outs[now].start()
    for copy in outs:
        copy.wait()


def place(got, mate):
    return pl.pallas_call(
        place_kernel,
        out_shape=jax.ShapeDtypeStruct((864, 256), f32),
        in_specs=[vmem(), vmem()],
        out_specs=hbm(),
        scratch_shapes=[pltpu.VMEM((896, 256), f32), pltpu.SemaphoreType.DMA((7,))],
        compiler_params=params(8),
    )(got, mate)


def body(features, grad_out, weight, neighbours):
    x = features[0, 0]
    c = grad_out[0, 0]
    links = jnp.maximum(neighbours[0, 0], -1)
    mates = [(i, i ^ 1) for i in range(SPACE)]
    same_core = [[2 * q + core for q in range(CHIPS)] for core in range(2)]
    grad_scale = 1.0 / math.sqrt(SCENES * SPACE * 512)

    mate_links, mate_x, mate_c = [lax.ppermute(rows, "space", mates) for rows in (links, x, c)]
    own = jnp.concatenate([x, c], axis=1)
    outgoing = pack(links, mate_links, own, mate_x, mate_c)
    halos = []
    for hop, rows in enumerate(outgoing, 1):
        up = [(2 * q, 2 * (q + hop)) for q in range(CHIPS - hop)]
        down = [(2 * (q + hop) + 1, 2 * q + 1) for q in range(CHIPS - hop)]
        halos.append(lax.ppermute(rows, "space", up + down))
    here, turned, x_half, c_half = stage(links, mate_links, own, mate_x, mate_c, outgoing[3])
    *halos, here, turned, x_half, c_half = lax.optimization_barrier((*halos, here, turned, x_half, c_half))
    halos += [lax.ppermute(rows, "space", mates) for rows in halos] + [here]
    terms = kernel_grad(links, mate_links, c_half, turned, halos)
    got_terms = lax.all_to_all(terms, "space", 0, 0, tiled=True, axis_index_groups=same_core)
    grad_in, mate_grad_in = taps_product(True, links, mate_links, c_half, weight, halos, terms)
    conv_out, mate_conv_out = taps_product(False, links, mate_links, x_half, weight, halos, terms)
    got_terms, grad_in, mate_grad_in, conv_out, mate_conv_out = lax.optimization_barrier(
        (got_terms, grad_in, mate_grad_in, conv_out, mate_conv_out)
    )
    scene_terms = lax.all_to_all(scene_sum(got_terms), "dp", 0, 0, tiled=True)
    whole = whole_sum(grad_scale, scene_terms)
    whole = lax.all_to_all(whole, "space", 0, 0, tiled=True, axis_index_groups=same_core)
    mate_whole = lax.ppermute(whole, "space", mates)
    grad_in = (grad_in + lax.ppermute(mate_grad_in, "space", mates)).astype(bf16)
    conv_out = (conv_out + lax.ppermute(mate_conv_out, "space", mates)).astype(bf16)
    return conv_out[None, None], grad_in[None, None], place(whole, mate_whole)


def solution(mesh):
    placed = (
        P("dp", "space", None, None),
        P("dp", "space", None, None),
        P(),
        P("dp", "space", None),
    )
    return jax.shard_map(
        body,
        mesh=mesh,
        in_specs=placed,
        out_specs=(P("dp", "space", None, None), P("dp", "space", None, None), P("dp", None)),
        check_vma=False,
    )
```

```python
import functools
import math

import jax
import jax.numpy as jnp
from jax import lax
from jax.experimental import pallas as pl
from jax.experimental.pallas import tpu as pltpu
from jax.sharding import PartitionSpec as P

f32 = jnp.float32
bf16 = jnp.bfloat16
i16 = jnp.int16
i32 = jnp.int32

SPACE = 32
LG, LS, LW, LP, LQ = 51, 50, 50, 51, 51

SCENES = 8
CHIPS = 16
HALF = 128
LEVELS = 32766.0

ROWS = (256, 192, 64, 16)
FIRST = (0, 256, 448, 512)
BELOW = 528
HERE = 1056

OFFSETS = [(k, k // 9 - 1, k // 3 % 3 - 1, k % 3 - 1) for k in range(27) if k != 13]


def position():
    return lax.axis_index("space"), lax.axis_index("dp")


def params(mib):
    return pltpu.CompilerParams(vmem_limit_bytes=mib << 20)


def cost(us):
    return pl.CostEstimate(flops=int(us * 1e9), bytes_accessed=1 << 20, transcendentals=0)


def vmem():
    return pl.BlockSpec(memory_space=pltpu.VMEM)


def smem():
    return pl.BlockSpec(memory_space=pltpu.SMEM)


def hbm():
    return pl.BlockSpec(memory_space=pltpu.HBM)


def anywhere():
    return pl.BlockSpec(memory_space=pl.ANY)


def side(shift):
    return 7 if shift > 0 else 0


def region(ref, shifts):
    dx, dy, dz = shifts
    kinds = (dx != 0, dy != 0, dz != 0)
    if kinds == (True, False, False):
        return ref[pl.ds(side(dx) * 64, 64), :]
    if kinds == (False, True, False):
        return jnp.concatenate([ref[pl.ds(x * 64 + side(dy) * 8, 8), :] for x in range(8)], axis=0)
    if kinds == (False, False, True):
        return ref[pl.ds(side(dz), 64, stride=8), :]
    if kinds == (True, True, False):
        rows = ref[pl.ds(side(dx) * 64 + side(dy) * 8, 8), :]
    elif kinds == (True, False, True):
        rows = ref[pl.ds(side(dx) * 64 + side(dz), 8, stride=8), :]
    elif kinds == (False, True, True):
        rows = ref[pl.ds(side(dy) * 8 + side(dz), 8, stride=64), :]
    else:
        row = ref[pl.ds(side(dx) * 64 + side(dy) * 8 + side(dz), 1), :]
        rows = jnp.broadcast_to(row, (8, HALF))
    return jnp.concatenate([rows, rows], axis=0)


def is_face(shifts):
    return sum(map(abs, shifts)) == 1


def reach(shifts):
    return abs(shifts[0] + 2 * shifts[1] + 4 * shifts[2])


def place_in_slots(distance, shifts, source, target):
    if distance <= 1:
        return 64 * (2 * source + target)
    if distance == 2:
        return 96 * source + (0 if is_face(shifts) else 64 + 16 * target)
    return 16 * (2 * source + target) if distance == 3 else 0


def pack_kernel(links_ref, mate_links_ref, own_ref, mate_x_ref, mate_c_ref, *rest):
    outs, parts = rest[:4], rest[4]
    own = position()[0]
    core = lax.rem(own, 2)
    chip = own // 2
    for group in range(4):
        lanes = slice(group * HALF, (group + 1) * HALF)
        parts[core, group] = own_ref[:, lanes].astype(f32)
        mate_ref, at = (mate_x_ref, lanes) if group < 2 else (mate_c_ref, slice(lanes.start - 256, lanes.stop - 256))
        parts[1 - core, group] = mate_ref[:, at].astype(f32)
    for brick in range(2):
        for k, *shifts in OFFSETS:
            target = jnp.where(core == brick, links_ref[k], mate_links_ref[k])
            distance = (target // 2 - chip) * (1 - 2 * core)
            to = lax.rem(target, 2)

            @pl.when((target >= 0) & (distance > 0))
            def _(brick=brick, distance=distance, to=to, shifts=tuple(shifts)):
                for step in range(1, 5):
                    if reach(shifts) >= 2 * step - 1:

                        @pl.when(distance == step)
                        def _(step=step):
                            at = pl.multiple_of(place_in_slots(step, shifts, brick, to), 16)
                            for group in range(4):
                                rows = region(parts.at[brick, group], shifts)
                                lanes = slice(group * HALF, (group + 1) * HALF)
                                outs[step - 1][pl.ds(at, rows.shape[0]), lanes] = rows.astype(bf16)


def pack(links, mate_links, own, mate_x, mate_c):
    return pl.pallas_call(
        pack_kernel,
        out_shape=tuple(jax.ShapeDtypeStruct((rows, 512), bf16) for rows in ROWS),
        in_specs=[smem(), smem()] + [vmem()] * 3,
        out_specs=(vmem(),) * 4,
        scratch_shapes=[pltpu.VMEM((2, 4, 512, HALF), f32)],
        compiler_params=params(LQ),
        cost_estimate=cost(2.5),
    )(links, mate_links, own, mate_x, mate_c)


def stage_kernel(
    links_ref, mate_links_ref, own_ref, mate_x_ref, mate_c_ref, _, here_ref, turned_ref, x_half_ref, c_half_ref, parts
):
    own = position()[0]
    core = lax.rem(own, 2)
    for here in range(2):

        @pl.when(core == here)
        def _(here=here):
            lanes = slice(here * HALF, (here + 1) * HALF)
            x_half_ref[here] = own_ref[:, lanes]
            x_half_ref[1 - here] = mate_x_ref[:, lanes]
            c_half_ref[here] = own_ref[:, 256 + here * HALF : 256 + (here + 1) * HALF]
            c_half_ref[1 - here] = mate_c_ref[:, lanes]

    for brick in range(2):
        parts[brick, 0] = x_half_ref[brick].astype(f32)
        parts[brick, 1] = c_half_ref[brick].astype(f32)
        for k, *shifts in OFFSETS:
            target = jnp.where(core == brick, links_ref[k], mate_links_ref[k])

            @pl.when((target >= 0) & (target // 2 == own // 2))
            def _(brick=brick, target=target, shifts=tuple(shifts)):
                at = pl.multiple_of(place_in_slots(0, shifts, brick, lax.rem(target, 2)), 16)
                for tensor in range(2):
                    rows = region(parts.at[brick, tensor], shifts)
                    here_ref[pl.ds(at, rows.shape[0]), tensor * HALF : (tensor + 1) * HALF] = rows.astype(bf16)

    turned_ref[core] = own_ref[:, 0:256].T
    turned_ref[1 - core] = mate_x_ref[...].T


def stage(links, mate_links, own, mate_x, mate_c, after):
    half = jax.ShapeDtypeStruct((2, 512, HALF), bf16)
    return pl.pallas_call(
        stage_kernel,
        out_shape=(
            jax.ShapeDtypeStruct((256, 256), bf16),
            jax.ShapeDtypeStruct((2, 256, 512), bf16),
            half,
            half,
        ),
        in_specs=[smem(), smem()] + [vmem()] * 3 + [anywhere()],
        out_specs=(vmem(),) * 4,
        scratch_shapes=[pltpu.VMEM((2, 2, 512, HALF), f32)],
        compiler_params=params(LP),
        cost_estimate=cost(1.5),
    )(links, mate_links, own, mate_x, mate_c, after)


def target_plane(shift):
    return 9 if shift > 0 else 0


def scaling(peak):
    code = jnp.ceil(jnp.log2(jnp.maximum(peak, 2.0**-110)) * 256.0) + 1.0
    return LEVELS * jnp.exp2(code * (-1.0 / 256.0)), code


def fixed(values):
    return jnp.round(values).astype(i32).astype(i16)


def plain(coded):
    return coded.astype(i32).astype(f32)


def step_of(code):
    return jnp.exp2(code * (1.0 / 256.0)) * (1.0 / LEVELS)


def fill(brick, links, fetch, ready, own_rows, plane, low, high, shifted_low, shifted_high, padded):
    plane[...] = jnp.zeros_like(plane)
    low[...] = jnp.zeros_like(low)
    high[...] = jnp.zeros_like(high)
    for x in range(8):
        plane[pl.ds((x + 1) * 80 + 8, 64), :] = own_rows(x * 64)
    for copy in ready:
        copy.wait()
    for k, dx, dy, dz in OFFSETS:
        source = links[k]

        @pl.when(source >= 0)
        def _(source=source, dx=dx, dy=dy, dz=dz):
            at_x, at_y = target_plane(dx), target_plane(dy)
            face = (dx != 0) + (dy != 0) + (dz != 0) == 1
            got = fetch(source, brick, (dx, dy, dz), 64 if face else 16).astype(f32)
            if dz == 0:
                if dy == 0:
                    plane[pl.ds(at_x * 80 + 8, 64), :] = got
                elif dx == 0:
                    for x in range(8):
                        plane[pl.ds((x + 1) * 80 + at_y * 8, 8), :] = got[x * 8 : x * 8 + 8]
                else:
                    plane[pl.ds(at_x * 80 + at_y * 8, 8), :] = got[0:8]
            else:
                rim = low if dz < 0 else high
                if dx == 0 and dy == 0:
                    for x in range(8):
                        rim[pl.ds((x + 1) * 10 + 1, 8), :] = got[x * 8 : x * 8 + 8]
                elif dy == 0:
                    rim[pl.ds(at_x * 10 + 1, 8), :] = got[0:8]
                elif dx == 0:
                    rim[pl.ds(10 + at_y, 8, stride=10), :] = got[0:8]
                else:
                    rim[pl.ds(at_x * 10 + at_y, 1), :] = got[0:1]

    shifted_low[pl.ds(1, 800), :] = plane[pl.ds(0, 800), :]
    shifted_low[pl.ds(0, 104, stride=8), :] = low[...]
    shifted_high[pl.ds(0, 800), :] = plane[pl.ds(1, 800), :]
    shifted_high[pl.ds(7, 104, stride=8), :] = high[...]
    for j in range(3):
        for l, source in enumerate((shifted_low, plane, shifted_high)):
            at = (3 * j + l) * HALF
            for x in range(10):
                padded[brick, x * 64 : x * 64 + 64, at : at + HALF] = source[pl.ds(x * 80 + j * 8, 64), :].astype(bf16)


def fill_both(core, links_ref, mate_links_ref, half_ref, halo_copies, fetch, scratch):
    for brick in range(2):

        def rows(first, brick=brick):
            return half_ref[brick, pl.ds(first, 64), :].astype(f32)

        links = [jnp.where(core == brick, links_ref[k], mate_links_ref[k]) for k in range(27)]
        fill(brick, links, fetch, halo_copies if brick == 0 else [], rows, *scratch)


def take_halos(tensor, own, halos, slots, sems):
    core = lax.rem(own, 2)
    chip = own // 2
    lanes = pl.ds(pl.multiple_of(2 * tensor * HALF + core * HALF, HALF), HALF)
    copies = []
    for n, (halo, rows, first) in enumerate(zip(halos[:8], ROWS * 2, FIRST * 2)):
        side = (1 - core) if n < 4 else core
        at = pl.multiple_of(side * BELOW + first, 16)
        copies.append(pltpu.make_async_copy(halo.at[:, lanes], slots.at[pl.ds(at, rows), :], sems.at[n]))
    copies.append(
        pltpu.make_async_copy(halos[8].at[:, pl.ds(tensor * HALF, HALF)], slots.at[pl.ds(HERE, 256), :], sems.at[8])
    )

    def fetch(source, brick, shifts, count):
        apart = source // 2 - chip
        distance = jnp.abs(apart)
        source = lax.rem(source, 2)
        at = HERE + place_in_slots(0, shifts, source, brick)
        for step in range(1, 5):
            if reach(shifts) >= 2 * step - 1:
                there = FIRST[step - 1] + place_in_slots(step, shifts, source, brick)
                at = jnp.where(distance == step, there + jnp.where(apart < 0, BELOW, 0), at)
        return slots[pl.ds(pl.multiple_of(at, 16), count), :]

    return copies, fetch


HALO_SCRATCH = [pltpu.VMEM((HERE + 256, HALF), bf16), pltpu.SemaphoreType.DMA((9,))]
FILL_SCRATCH = [
    pltpu.VMEM((832, HALF), f32),
    pltpu.VMEM((104, HALF), f32),
    pltpu.VMEM((104, HALF), f32),
    pltpu.VMEM((832, HALF), f32),
    pltpu.VMEM((832, HALF), f32),
    pltpu.VMEM((2, 640, 9 * HALF), bf16),
]


def kernel_grad_kernel(links_ref, mate_links_ref, c_half_ref, turned_ref, *rest):
    halos, (terms_ref, grads, coded, sems, slots, halo_sems, *scratch) = rest[:9], rest[9:]
    own = position()[0]
    padded = scratch[-1]
    halo_copies, fetch = take_halos(1, own, halos, slots, halo_sems)
    for copy in halo_copies:
        copy.start()
    fill_both(lax.rem(own, 2), links_ref, mate_links_ref, c_half_ref, halo_copies, fetch, scratch)
    for i in range(3):
        window = slice(i * 64, i * 64 + 512)
        term = jnp.dot(turned_ref[0], padded[0, window, :], preferred_element_type=f32)
        term += jnp.dot(turned_ref[1], padded[1, window, :], preferred_element_type=f32)
        for jl in range(9):
            grads[26 - (9 * i + jl)] = term[:, jl * HALF : (jl + 1) * HALF]
    copies = []
    for q in range(CHIPS):
        def rows(k, q=q):
            return jnp.concatenate([grads[k, pl.ds(at + q * 8, 8), :] for at in (0, 128)], axis=0)

        peak = jnp.abs(rows(0))
        for k in range(1, 27):
            peak = jnp.maximum(peak, jnp.abs(rows(k)))
        factor, code = scaling(jnp.max(peak, axis=0, keepdims=True))
        for k in range(27):
            coded[q, k * 16 : k * 16 + 16, :] = fixed(rows(k) * factor)
        coded[q, 432:448, :] = fixed(jnp.broadcast_to(code, (16, HALF)))
        copies.append(pltpu.make_async_copy(coded.at[q], terms_ref.at[q], sems.at[q]))
        copies[-1].start()
    for copy in copies:
        copy.wait()


def kernel_grad(links, mate_links, c_half, turned, halos):
    return pl.pallas_call(
        kernel_grad_kernel,
        out_shape=jax.ShapeDtypeStruct((CHIPS, 448, HALF), i16),
        in_specs=[smem(), smem(), vmem(), vmem()] + [anywhere()] * 9,
        out_specs=anywhere(),
        scratch_shapes=[
            pltpu.VMEM((27, 256, HALF), f32),
            pltpu.VMEM((CHIPS, 448, HALF), i16),
            pltpu.SemaphoreType.DMA((CHIPS,)),
        ]
        + HALO_SCRATCH
        + FILL_SCRATCH,
        compiler_params=params(LG),
        cost_estimate=cost(6.0),
    )(links, mate_links, c_half, turned, *halos)


def taps_kernel(turned, links_ref, mate_links_ref, half_ref, weight_ref, *rest):
    halos, (_, out_ref, mate_out_ref, taps, sems, slots, halo_sems, *scratch) = rest[:9], rest[9:]
    own = position()[0]
    core = lax.rem(own, 2)
    start = pl.multiple_of(core * HALF, HALF)
    halo_copies, fetch = take_halos(1 if turned else 0, own, halos, slots, halo_sems)
    if turned:
        copies = [
            pltpu.make_async_copy(
                weight_ref.at[26 - k, :, pl.ds(start, HALF)], taps.at[:, pl.ds(k * HALF, HALF)], sems.at[k]
            )
            for k in range(27)
        ]
    else:
        copies = [pltpu.make_async_copy(weight_ref.at[:, pl.ds(start, HALF), :], taps, sems.at[0])]
    padded = scratch[-1]
    for copy in halo_copies + copies:
        copy.start()
    fill_both(core, links_ref, mate_links_ref, half_ref, halo_copies, fetch, scratch)
    for copy in copies:
        copy.wait()
    for to_mate, out in ((0, out_ref), (1, mate_out_ref)):
        brick = lax.rem(core + to_mate, 2)
        total = jnp.zeros((512, 256), f32)
        for i in range(3):
            block = padded[brick, i * 64 : i * 64 + 512, :]
            if turned:
                now = taps[:, i * 9 * HALF : (i + 1) * 9 * HALF]
                total += lax.dot_general(block, now, (((1,), (1,)), ((), ())), preferred_element_type=f32)
            else:
                now = taps[9 * i : 9 * i + 9].reshape(9 * HALF, 256)
                total += jnp.dot(block, now, preferred_element_type=f32)
        out[...] = total


def taps_product(turned, links, mate_links, half, weight, halos, after):
    taps = pltpu.VMEM((256, 27 * HALF) if turned else (27, HALF, 256), bf16)
    return pl.pallas_call(
        functools.partial(taps_kernel, turned),
        out_shape=(jax.ShapeDtypeStruct((512, 256), f32),) * 2,
        in_specs=[smem(), smem(), vmem(), hbm()] + [anywhere()] * 10,
        out_specs=(vmem(), vmem()),
        scratch_shapes=[taps, pltpu.SemaphoreType.DMA((27,))] + HALO_SCRATCH + FILL_SCRATCH,
        compiler_params=params(56),
        cost_estimate=cost(6.0),
    )(links, mate_links, half, weight, *halos, after)


def first_unit(chip, scene):
    return lax.rem(chip - 12 * scene + 96, 16)


def coded_block(values):
    factor, code = scaling(jnp.max(jnp.abs(values), axis=0, keepdims=True))
    return fixed(jnp.concatenate([values * factor, jnp.broadcast_to(code, (8, HALF))], axis=0))


def plain_block(coded):
    values = plain(coded)
    return values[0:56] * step_of(values[56:57])


def scene_kernel(got_ref, out_ref, total):
    chip = position()[0] // 2
    steps = [step_of(plain(got_ref[source, 432:448, :])) for source in range(CHIPS)]
    for k in range(27):
        sums = jnp.zeros((16, HALF), f32)
        for source in range(CHIPS):
            sums += plain(got_ref[source, k * 16 : k * 16 + 16, :]) * steps[source]
        total[2 * k] = sums[0:8]
        total[2 * k + 1] = sums[8:16]
    total[54] = jnp.zeros((8, HALF), f32)
    for scene in range(SCENES):
        first = (108 * scene + first_unit(chip, scene) - chip) // 16
        units = [total[jnp.minimum(first + t, 54)] for t in range(7)]
        out_ref[scene] = coded_block(jnp.concatenate(units, axis=0))


def scene_sum(got):
    return pl.pallas_call(
        scene_kernel,
        out_shape=jax.ShapeDtypeStruct((SCENES, 64, HALF), i16),
        in_specs=[vmem()],
        out_specs=vmem(),
        scratch_shapes=[pltpu.VMEM((55, 8, HALF), f32)],
        compiler_params=params(LS),
        cost_estimate=cost(2.5),
    )(got)


def whole_kernel(scale, got_ref, out_ref):
    total = plain_block(got_ref[0])
    for scene in range(1, SCENES):
        total += plain_block(got_ref[scene])
    block = coded_block(total * scale)
    for target in range(CHIPS):
        out_ref[target] = block


def whole_sum(scale, got):
    return pl.pallas_call(
        functools.partial(whole_kernel, scale),
        out_shape=jax.ShapeDtypeStruct((CHIPS, 64, HALF), i16),
        in_specs=[vmem()],
        out_specs=vmem(),
        compiler_params=params(LW),
        cost_estimate=cost(1.5),
    )(got)


def place_kernel(got_ref, mate_ref, out_ref, whole, sems):
    space, scene = position()
    core = lax.rem(space, 2)
    outs = [
        pltpu.make_async_copy(whole.at[pl.ds(t * 128, size), :], out_ref.at[pl.ds(t * 128, size), :], sems.at[t])
        for t, size in enumerate((128,) * 6 + (96,))
    ]
    both = ((got_ref, pl.multiple_of(core * HALF, HALF)), (mate_ref, pl.multiple_of((1 - core) * HALF, HALF)))
    steps = [[step_of(plain(ref[chip, 48:64, :])[8:9]) for chip in range(CHIPS)] for ref, _ in both]
    for t in range(0, 7, 2):
        for chip in range(CHIPS):
            rest = first_unit(chip, scene)
            for n, (ref, at_lane) in enumerate(both):
                values = plain(ref[chip, t * 8 : t * 8 + 16, :]) * steps[n][chip]
                for now in range(t, min(t + 2, 7)):
                    at = pl.multiple_of((16 * now + rest) * 8, 8)
                    whole[pl.ds(at, 8), pl.ds(at_lane, HALF)] = values[(now - t) * 8 : (now - t + 1) * 8]
        for now in range(t, min(t + 2, 7)):
            outs[now].start()
    for copy in outs:
        copy.wait()


def place(got, mate):
    return pl.pallas_call(
        place_kernel,
        out_shape=jax.ShapeDtypeStruct((864, 256), f32),
        in_specs=[vmem(), vmem()],
        out_specs=hbm(),
        scratch_shapes=[pltpu.VMEM((896, 256), f32), pltpu.SemaphoreType.DMA((7,))],
        compiler_params=params(8),
    )(got, mate)


def body(features, grad_out, weight, neighbours):
    x = features[0, 0]
    c = grad_out[0, 0]
    links = jnp.maximum(neighbours[0, 0], -1)
    mates = [(i, i ^ 1) for i in range(SPACE)]
    same_core = [[2 * q + core for q in range(CHIPS)] for core in range(2)]
    grad_scale = 1.0 / math.sqrt(SCENES * SPACE * 512)

    mate_links, mate_x, mate_c = [lax.ppermute(rows, "space", mates) for rows in (links, x, c)]
    own = jnp.concatenate([x, c], axis=1)
    outgoing = pack(links, mate_links, own, mate_x, mate_c)
    halos = []
    for hop, rows in enumerate(outgoing, 1):
        up = [(2 * q, 2 * (q + hop)) for q in range(CHIPS - hop)]
        down = [(2 * (q + hop) + 1, 2 * q + 1) for q in range(CHIPS - hop)]
        halos.append(lax.ppermute(rows, "space", up + down))
    here, turned, x_half, c_half = stage(links, mate_links, own, mate_x, mate_c, outgoing[3])
    *halos, here, turned, x_half, c_half = lax.optimization_barrier((*halos, here, turned, x_half, c_half))
    halos += [lax.ppermute(rows, "space", mates) for rows in halos] + [here]
    terms = kernel_grad(links, mate_links, c_half, turned, halos)
    got_terms = lax.all_to_all(terms, "space", 0, 0, tiled=True, axis_index_groups=same_core)
    grad_in, mate_grad_in = taps_product(True, links, mate_links, c_half, weight, halos, terms)
    conv_out, mate_conv_out = taps_product(False, links, mate_links, x_half, weight, halos, terms)
    grad_in = (grad_in + lax.ppermute(mate_grad_in, "space", mates)).astype(bf16)
    conv_out = (conv_out + lax.ppermute(mate_conv_out, "space", mates)).astype(bf16)
    got_terms, grad_in, conv_out = lax.optimization_barrier((got_terms, grad_in, conv_out))
    scene_terms = lax.all_to_all(scene_sum(got_terms), "dp", 0, 0, tiled=True)
    whole = whole_sum(grad_scale, scene_terms)
    whole = lax.all_to_all(whole, "space", 0, 0, tiled=True, axis_index_groups=same_core)
    mate_whole = lax.ppermute(whole, "space", mates)
    return conv_out[None, None], grad_in[None, None], place(whole, mate_whole)


def solution(mesh):
    placed = (
        P("dp", "space", None, None),
        P("dp", "space", None, None),
        P(),
        P("dp", "space", None),
    )
    return jax.shard_map(
        body,
        mesh=mesh,
        in_specs=placed,
        out_specs=(P("dp", "space", None, None), P("dp", "space", None, None), P("dp", None)),
        check_vma=False,
    )
```

```python
import functools
import math

import jax
import jax.numpy as jnp
from jax import lax
from jax.experimental import pallas as pl
from jax.experimental.pallas import tpu as pltpu
from jax.sharding import PartitionSpec as P

f32 = jnp.float32
bf16 = jnp.bfloat16
i16 = jnp.int16
i32 = jnp.int32

SPACE = 32
LG, LS, LW, LP, LQ = 51, 50, 50, 51, 51

SCENES = 8
CHIPS = 16
HALF = 128
LEVELS = 32766.0

ROWS = (256, 192, 64, 16)
FIRST = (0, 256, 448, 512)
BELOW = 528
HERE = 1056

OFFSETS = [(k, k // 9 - 1, k // 3 % 3 - 1, k % 3 - 1) for k in range(27) if k != 13]


def position():
    return lax.axis_index("space"), lax.axis_index("dp")


def params(mib):
    return pltpu.CompilerParams(vmem_limit_bytes=mib << 20)


def cost(us):
    return pl.CostEstimate(flops=int(us * 1e9), bytes_accessed=1 << 20, transcendentals=0)


def vmem():
    return pl.BlockSpec(memory_space=pltpu.VMEM)


def smem():
    return pl.BlockSpec(memory_space=pltpu.SMEM)


def hbm():
    return pl.BlockSpec(memory_space=pltpu.HBM)


def anywhere():
    return pl.BlockSpec(memory_space=pl.ANY)


def side(shift):
    return 7 if shift > 0 else 0


def region(ref, shifts):
    dx, dy, dz = shifts
    kinds = (dx != 0, dy != 0, dz != 0)
    if kinds == (True, False, False):
        return ref[pl.ds(side(dx) * 64, 64), :]
    if kinds == (False, True, False):
        return jnp.concatenate([ref[pl.ds(x * 64 + side(dy) * 8, 8), :] for x in range(8)], axis=0)
    if kinds == (False, False, True):
        return ref[pl.ds(side(dz), 64, stride=8), :]
    if kinds == (True, True, False):
        rows = ref[pl.ds(side(dx) * 64 + side(dy) * 8, 8), :]
    elif kinds == (True, False, True):
        rows = ref[pl.ds(side(dx) * 64 + side(dz), 8, stride=8), :]
    elif kinds == (False, True, True):
        rows = ref[pl.ds(side(dy) * 8 + side(dz), 8, stride=64), :]
    else:
        row = ref[pl.ds(side(dx) * 64 + side(dy) * 8 + side(dz), 1), :]
        rows = jnp.broadcast_to(row, (8, HALF))
    return jnp.concatenate([rows, rows], axis=0)


def is_face(shifts):
    return sum(map(abs, shifts)) == 1


def reach(shifts):
    return abs(shifts[0] + 2 * shifts[1] + 4 * shifts[2])


def place_in_slots(distance, shifts, source, target):
    if distance <= 1:
        return 64 * (2 * source + target)
    if distance == 2:
        return 96 * source + (0 if is_face(shifts) else 64 + 16 * target)
    return 16 * (2 * source + target) if distance == 3 else 0


def pack_kernel(links_ref, mate_links_ref, own_ref, mate_x_ref, mate_c_ref, *rest):
    outs, parts = rest[:4], rest[4]
    own = position()[0]
    core = lax.rem(own, 2)
    chip = own // 2
    for group in range(4):
        lanes = slice(group * HALF, (group + 1) * HALF)
        parts[core, group, 0:512, :] = own_ref[:, lanes].astype(f32)
        mate_ref, at = (mate_x_ref, lanes) if group < 2 else (mate_c_ref, slice(lanes.start - 256, lanes.stop - 256))
        parts[1 - core, group, 0:512, :] = mate_ref[:, at].astype(f32)
    for brick in range(2):
        for k, *shifts in OFFSETS:
            target = jnp.where(core == brick, links_ref[k], mate_links_ref[k])
            distance = (target // 2 - chip) * (1 - 2 * core)
            to = lax.rem(target, 2)

            @pl.when((target >= 0) & (distance > 0))
            def _(brick=brick, distance=distance, to=to, shifts=tuple(shifts)):
                for step in range(1, 5):
                    if reach(shifts) >= 2 * step - 1:

                        @pl.when(distance == step)
                        def _(step=step):
                            at = pl.multiple_of(place_in_slots(step, shifts, brick, to), 16)
                            for group in range(4):
                                rows = region(parts.at[brick, group], shifts)
                                lanes = slice(group * HALF, (group + 1) * HALF)
                                outs[step - 1][pl.ds(at, rows.shape[0]), lanes] = rows.astype(bf16)


def pack(links, mate_links, own, mate_x, mate_c):
    return pl.pallas_call(
        pack_kernel,
        out_shape=tuple(jax.ShapeDtypeStruct((rows, 512), bf16) for rows in ROWS),
        in_specs=[smem(), smem()] + [vmem()] * 3,
        out_specs=(vmem(),) * 4,
        scratch_shapes=[pltpu.VMEM((2, 4, 576, HALF), f32)],
        compiler_params=params(LQ),
        cost_estimate=cost(2.5),
    )(links, mate_links, own, mate_x, mate_c)


def stage_kernel(
    links_ref, mate_links_ref, own_ref, mate_x_ref, mate_c_ref, _, here_ref, turned_ref, x_half_ref, c_half_ref, parts
):
    own = position()[0]
    core = lax.rem(own, 2)
    for here in range(2):

        @pl.when(core == here)
        def _(here=here):
            lanes = slice(here * HALF, (here + 1) * HALF)
            x_half_ref[here] = own_ref[:, lanes]
            x_half_ref[1 - here] = mate_x_ref[:, lanes]
            c_half_ref[here] = own_ref[:, 256 + here * HALF : 256 + (here + 1) * HALF]
            c_half_ref[1 - here] = mate_c_ref[:, lanes]

    for brick in range(2):
        parts[brick, 0, 0:512, :] = x_half_ref[brick].astype(f32)
        parts[brick, 1, 0:512, :] = c_half_ref[brick].astype(f32)
        for k, *shifts in OFFSETS:
            target = jnp.where(core == brick, links_ref[k], mate_links_ref[k])

            @pl.when((target >= 0) & (target // 2 == own // 2))
            def _(brick=brick, target=target, shifts=tuple(shifts)):
                at = pl.multiple_of(place_in_slots(0, shifts, brick, lax.rem(target, 2)), 16)
                for tensor in range(2):
                    rows = region(parts.at[brick, tensor], shifts)
                    here_ref[pl.ds(at, rows.shape[0]), tensor * HALF : (tensor + 1) * HALF] = rows.astype(bf16)

    turned_ref[core] = own_ref[:, 0:256].T
    turned_ref[1 - core] = mate_x_ref[...].T


def stage(links, mate_links, own, mate_x, mate_c, after):
    half = jax.ShapeDtypeStruct((2, 512, HALF), bf16)
    return pl.pallas_call(
        stage_kernel,
        out_shape=(
            jax.ShapeDtypeStruct((256, 256), bf16),
            jax.ShapeDtypeStruct((2, 256, 512), bf16),
            half,
            half,
        ),
        in_specs=[smem(), smem()] + [vmem()] * 3 + [anywhere()],
        out_specs=(vmem(),) * 4,
        scratch_shapes=[pltpu.VMEM((2, 2, 576, HALF), f32)],
        compiler_params=params(LP),
        cost_estimate=cost(1.5),
    )(links, mate_links, own, mate_x, mate_c, after)


def target_plane(shift):
    return 9 if shift > 0 else 0


def scaling(peak):
    code = jnp.ceil(jnp.log2(jnp.maximum(peak, 2.0**-110)) * 256.0) + 1.0
    return LEVELS * jnp.exp2(code * (-1.0 / 256.0)), code


def fixed(values):
    return jnp.round(values).astype(i32).astype(i16)


def plain(coded):
    return coded.astype(i32).astype(f32)


def step_of(code):
    return jnp.exp2(code * (1.0 / 256.0)) * (1.0 / LEVELS)


def fill(brick, links, fetch, ready, own_rows, plane, low, high, shifted_low, shifted_high, padded):
    plane[...] = jnp.zeros_like(plane)
    low[...] = jnp.zeros_like(low)
    high[...] = jnp.zeros_like(high)
    for x in range(8):
        plane[pl.ds((x + 1) * 80 + 8, 64), :] = own_rows(x * 64)
    for copy in ready:
        copy.wait()
    for k, dx, dy, dz in OFFSETS:
        source = links[k]

        @pl.when(source >= 0)
        def _(source=source, dx=dx, dy=dy, dz=dz):
            at_x, at_y = target_plane(dx), target_plane(dy)
            face = (dx != 0) + (dy != 0) + (dz != 0) == 1
            got = fetch(source, brick, (dx, dy, dz), 64 if face else 16).astype(f32)
            if dz == 0:
                if dy == 0:
                    plane[pl.ds(at_x * 80 + 8, 64), :] = got
                elif dx == 0:
                    for x in range(8):
                        plane[pl.ds((x + 1) * 80 + at_y * 8, 8), :] = got[x * 8 : x * 8 + 8]
                else:
                    plane[pl.ds(at_x * 80 + at_y * 8, 8), :] = got[0:8]
            else:
                rim = low if dz < 0 else high
                if dx == 0 and dy == 0:
                    for x in range(8):
                        rim[pl.ds((x + 1) * 10 + 1, 8), :] = got[x * 8 : x * 8 + 8]
                elif dy == 0:
                    rim[pl.ds(at_x * 10 + 1, 8), :] = got[0:8]
                elif dx == 0:
                    rim[pl.ds(10 + at_y, 8, stride=10), :] = got[0:8]
                else:
                    rim[pl.ds(at_x * 10 + at_y, 1), :] = got[0:1]

    shifted_low[pl.ds(1, 800), :] = plane[pl.ds(0, 800), :]
    shifted_low[pl.ds(0, 104, stride=8), :] = low[...]
    shifted_high[pl.ds(0, 800), :] = plane[pl.ds(1, 800), :]
    shifted_high[pl.ds(7, 104, stride=8), :] = high[...]
    for j in range(3):
        for l, source in enumerate((shifted_low, plane, shifted_high)):
            at = (3 * j + l) * HALF
            for x in range(10):
                padded[brick, x * 64 : x * 64 + 64, at : at + HALF] = source[pl.ds(x * 80 + j * 8, 64), :].astype(bf16)


def fill_both(core, links_ref, mate_links_ref, half_ref, halo_copies, fetch, scratch):
    for brick in range(2):

        def rows(first, brick=brick):
            return half_ref[brick, pl.ds(first, 64), :].astype(f32)

        links = [jnp.where(core == brick, links_ref[k], mate_links_ref[k]) for k in range(27)]
        fill(brick, links, fetch, halo_copies if brick == 0 else [], rows, *scratch)


def take_halos(tensor, own, halos, slots, sems):
    core = lax.rem(own, 2)
    chip = own // 2
    lanes = pl.ds(pl.multiple_of(2 * tensor * HALF + core * HALF, HALF), HALF)
    copies = []
    for n, (halo, rows, first) in enumerate(zip(halos[:8], ROWS * 2, FIRST * 2)):
        side = (1 - core) if n < 4 else core
        at = pl.multiple_of(side * BELOW + first, 16)
        copies.append(pltpu.make_async_copy(halo.at[:, lanes], slots.at[pl.ds(at, rows), :], sems.at[n]))
    copies.append(
        pltpu.make_async_copy(halos[8].at[:, pl.ds(tensor * HALF, HALF)], slots.at[pl.ds(HERE, 256), :], sems.at[8])
    )

    def fetch(source, brick, shifts, count):
        apart = source // 2 - chip
        distance = jnp.abs(apart)
        source = lax.rem(source, 2)
        at = HERE + place_in_slots(0, shifts, source, brick)
        for step in range(1, 5):
            if reach(shifts) >= 2 * step - 1:
                there = FIRST[step - 1] + place_in_slots(step, shifts, source, brick)
                at = jnp.where(distance == step, there + jnp.where(apart < 0, BELOW, 0), at)
        return slots[pl.ds(pl.multiple_of(at, 16), count), :]

    return copies, fetch


HALO_SCRATCH = [pltpu.VMEM((HERE + 256, HALF), bf16), pltpu.SemaphoreType.DMA((9,))]
FILL_SCRATCH = [
    pltpu.VMEM((840, HALF), f32),
    pltpu.VMEM((104, HALF), f32),
    pltpu.VMEM((104, HALF), f32),
    pltpu.VMEM((840, HALF), f32),
    pltpu.VMEM((840, HALF), f32),
    pltpu.VMEM((2, 640, 9 * HALF), bf16),
]


def kernel_grad_kernel(links_ref, mate_links_ref, c_half_ref, turned_ref, *rest):
    halos, (terms_ref, grads, coded, sems, slots, halo_sems, *scratch) = rest[:9], rest[9:]
    own = position()[0]
    padded = scratch[-1]
    halo_copies, fetch = take_halos(1, own, halos, slots, halo_sems)
    for copy in halo_copies:
        copy.start()
    fill_both(lax.rem(own, 2), links_ref, mate_links_ref, c_half_ref, halo_copies, fetch, scratch)
    for i in range(3):
        window = slice(i * 64, i * 64 + 512)
        term = jnp.dot(turned_ref[0], padded[0, window, :], preferred_element_type=f32)
        term += jnp.dot(turned_ref[1], padded[1, window, :], preferred_element_type=f32)
        for jl in range(9):
            grads[26 - (9 * i + jl)] = term[:, jl * HALF : (jl + 1) * HALF]
    copies = []
    for q in range(CHIPS):
        def rows(k, q=q):
            return jnp.concatenate([grads[k, pl.ds(at + q * 8, 8), :] for at in (0, 128)], axis=0)

        peak = jnp.abs(rows(0))
        for k in range(1, 27):
            peak = jnp.maximum(peak, jnp.abs(rows(k)))
        factor, code = scaling(jnp.max(peak, axis=0, keepdims=True))
        for k in range(27):
            coded[q, k * 16 : k * 16 + 16, :] = fixed(rows(k) * factor)
        coded[q, 432:448, :] = fixed(jnp.broadcast_to(code, (16, HALF)))
        copies.append(pltpu.make_async_copy(coded.at[q], terms_ref.at[q], sems.at[q]))
        copies[-1].start()
    for copy in copies:
        copy.wait()


def kernel_grad(links, mate_links, c_half, turned, halos):
    return pl.pallas_call(
        kernel_grad_kernel,
        out_shape=jax.ShapeDtypeStruct((CHIPS, 448, HALF), i16),
        in_specs=[smem(), smem(), vmem(), vmem()] + [anywhere()] * 9,
        out_specs=anywhere(),
        scratch_shapes=[
            pltpu.VMEM((27, 256, HALF), f32),
            pltpu.VMEM((CHIPS, 448, HALF), i16),
            pltpu.SemaphoreType.DMA((CHIPS,)),
        ]
        + HALO_SCRATCH
        + FILL_SCRATCH,
        compiler_params=params(LG),
        cost_estimate=cost(6.0),
    )(links, mate_links, c_half, turned, *halos)


def taps_kernel(turned, links_ref, mate_links_ref, half_ref, weight_ref, *rest):
    halos, (_, out_ref, mate_out_ref, taps, sems, slots, halo_sems, *scratch) = rest[:9], rest[9:]
    own = position()[0]
    core = lax.rem(own, 2)
    start = pl.multiple_of(core * HALF, HALF)
    halo_copies, fetch = take_halos(1 if turned else 0, own, halos, slots, halo_sems)
    if turned:
        copies = [
            pltpu.make_async_copy(
                weight_ref.at[26 - k, :, pl.ds(start, HALF)], taps.at[:, pl.ds(k * HALF, HALF)], sems.at[k]
            )
            for k in range(27)
        ]
    else:
        copies = [pltpu.make_async_copy(weight_ref.at[:, pl.ds(start, HALF), :], taps, sems.at[0])]
    padded = scratch[-1]
    for copy in halo_copies + copies:
        copy.start()
    fill_both(core, links_ref, mate_links_ref, half_ref, halo_copies, fetch, scratch)
    for copy in copies:
        copy.wait()
    for to_mate, out in ((0, out_ref), (1, mate_out_ref)):
        brick = lax.rem(core + to_mate, 2)
        total = jnp.zeros((512, 256), f32)
        for i in range(3):
            block = padded[brick, i * 64 : i * 64 + 512, :]
            if turned:
                now = taps[:, i * 9 * HALF : (i + 1) * 9 * HALF]
                total += lax.dot_general(block, now, (((1,), (1,)), ((), ())), preferred_element_type=f32)
            else:
                now = taps[9 * i : 9 * i + 9].reshape(9 * HALF, 256)
                total += jnp.dot(block, now, preferred_element_type=f32)
        out[...] = total


def taps_product(turned, links, mate_links, half, weight, halos, after):
    taps = pltpu.VMEM((256, 27 * HALF) if turned else (27, HALF, 256), bf16)
    return pl.pallas_call(
        functools.partial(taps_kernel, turned),
        out_shape=(jax.ShapeDtypeStruct((512, 256), f32),) * 2,
        in_specs=[smem(), smem(), vmem(), hbm()] + [anywhere()] * 10,
        out_specs=(vmem(), vmem()),
        scratch_shapes=[taps, pltpu.SemaphoreType.DMA((27,))] + HALO_SCRATCH + FILL_SCRATCH,
        compiler_params=params(56),
        cost_estimate=cost(6.0),
    )(links, mate_links, half, weight, *halos, after)


def first_unit(chip, scene):
    return lax.rem(chip - 12 * scene + 96, 16)


def coded_block(values):
    factor, code = scaling(jnp.max(jnp.abs(values), axis=0, keepdims=True))
    return fixed(jnp.concatenate([values * factor, jnp.broadcast_to(code, (8, HALF))], axis=0))


def plain_block(coded):
    values = plain(coded)
    return values[0:56] * step_of(values[56:57])


def scene_kernel(got_ref, out_ref, total):
    chip = position()[0] // 2
    steps = [step_of(plain(got_ref[source, 432:448, :])) for source in range(CHIPS)]
    for k in range(27):
        sums = jnp.zeros((16, HALF), f32)
        for source in range(CHIPS):
            sums += plain(got_ref[source, k * 16 : k * 16 + 16, :]) * steps[source]
        total[2 * k] = sums[0:8]
        total[2 * k + 1] = sums[8:16]
    total[54] = jnp.zeros((8, HALF), f32)
    for scene in range(SCENES):
        first = (108 * scene + first_unit(chip, scene) - chip) // 16
        units = [total[jnp.minimum(first + t, 54)] for t in range(7)]
        out_ref[scene] = coded_block(jnp.concatenate(units, axis=0))


def scene_sum(got):
    return pl.pallas_call(
        scene_kernel,
        out_shape=jax.ShapeDtypeStruct((SCENES, 64, HALF), i16),
        in_specs=[vmem()],
        out_specs=vmem(),
        scratch_shapes=[pltpu.VMEM((55, 8, HALF), f32)],
        compiler_params=params(LS),
        cost_estimate=cost(2.5),
    )(got)


def whole_kernel(scale, got_ref, out_ref):
    total = plain_block(got_ref[0])
    for scene in range(1, SCENES):
        total += plain_block(got_ref[scene])
    block = coded_block(total * scale)
    for target in range(CHIPS):
        out_ref[target] = block


def whole_sum(scale, got):
    return pl.pallas_call(
        functools.partial(whole_kernel, scale),
        out_shape=jax.ShapeDtypeStruct((CHIPS, 64, HALF), i16),
        in_specs=[vmem()],
        out_specs=vmem(),
        compiler_params=params(LW),
        cost_estimate=cost(1.5),
    )(got)


def place_kernel(got_ref, mate_ref, out_ref, whole, sems):
    space, scene = position()
    core = lax.rem(space, 2)
    outs = [
        pltpu.make_async_copy(whole.at[pl.ds(t * 128, size), :], out_ref.at[pl.ds(t * 128, size), :], sems.at[t])
        for t, size in enumerate((128,) * 6 + (96,))
    ]
    both = ((got_ref, pl.multiple_of(core * HALF, HALF)), (mate_ref, pl.multiple_of((1 - core) * HALF, HALF)))
    steps = [[step_of(plain(ref[chip, 48:64, :])[8:9]) for chip in range(CHIPS)] for ref, _ in both]
    for t in range(0, 7, 2):
        for chip in range(CHIPS):
            rest = first_unit(chip, scene)
            for n, (ref, at_lane) in enumerate(both):
                values = plain(ref[chip, t * 8 : t * 8 + 16, :]) * steps[n][chip]
                for now in range(t, min(t + 2, 7)):
                    at = pl.multiple_of((16 * now + rest) * 8, 8)
                    whole[pl.ds(at, 8), pl.ds(at_lane, HALF)] = values[(now - t) * 8 : (now - t + 1) * 8]
        for now in range(t, min(t + 2, 7)):
            outs[now].start()
    for copy in outs:
        copy.wait()


def place(got, mate):
    return pl.pallas_call(
        place_kernel,
        out_shape=jax.ShapeDtypeStruct((864, 256), f32),
        in_specs=[vmem(), vmem()],
        out_specs=hbm(),
        scratch_shapes=[pltpu.VMEM((896, 256), f32), pltpu.SemaphoreType.DMA((7,))],
        compiler_params=params(8),
    )(got, mate)


def body(features, grad_out, weight, neighbours):
    x = features[0, 0]
    c = grad_out[0, 0]
    links = jnp.maximum(neighbours[0, 0], -1)
    mates = [(i, i ^ 1) for i in range(SPACE)]
    same_core = [[2 * q + core for q in range(CHIPS)] for core in range(2)]
    grad_scale = 1.0 / math.sqrt(SCENES * SPACE * 512)

    mate_links, mate_x, mate_c = [lax.ppermute(rows, "space", mates) for rows in (links, x, c)]
    own = jnp.concatenate([x, c], axis=1)
    outgoing = pack(links, mate_links, own, mate_x, mate_c)
    halos = []
    for hop, rows in enumerate(outgoing, 1):
        up = [(2 * q, 2 * (q + hop)) for q in range(CHIPS - hop)]
        down = [(2 * (q + hop) + 1, 2 * q + 1) for q in range(CHIPS - hop)]
        halos.append(lax.ppermute(rows, "space", up + down))
    here, turned, x_half, c_half = stage(links, mate_links, own, mate_x, mate_c, outgoing[3])
    *halos, here, turned, x_half, c_half = lax.optimization_barrier((*halos, here, turned, x_half, c_half))
    halos += [lax.ppermute(rows, "space", mates) for rows in halos] + [here]
    terms = kernel_grad(links, mate_links, c_half, turned, halos)
    got_terms = lax.all_to_all(terms, "space", 0, 0, tiled=True, axis_index_groups=same_core)
    grad_in, mate_grad_in = taps_product(True, links, mate_links, c_half, weight, halos, terms)
    conv_out, mate_conv_out = taps_product(False, links, mate_links, x_half, weight, halos, terms)
    grad_in = (grad_in + lax.ppermute(mate_grad_in, "space", mates)).astype(bf16)
    conv_out = (conv_out + lax.ppermute(mate_conv_out, "space", mates)).astype(bf16)
    got_terms, grad_in, conv_out = lax.optimization_barrier((got_terms, grad_in, conv_out))
    scene_terms = lax.all_to_all(scene_sum(got_terms), "dp", 0, 0, tiled=True)
    whole = whole_sum(grad_scale, scene_terms)
    whole = lax.all_to_all(whole, "space", 0, 0, tiled=True, axis_index_groups=same_core)
    mate_whole = lax.ppermute(whole, "space", mates)
    return conv_out[None, None], grad_in[None, None], place(whole, mate_whole)


def solution(mesh):
    placed = (
        P("dp", "space", None, None),
        P("dp", "space", None, None),
        P(),
        P("dp", "space", None),
    )
    return jax.shard_map(
        body,
        mesh=mesh,
        in_specs=placed,
        out_specs=(P("dp", "space", None, None), P("dp", "space", None, None), P("dp", None)),
        check_vma=False,
    )
```
